128 devices in a mesh: gx: 2 (over y_hi), gy: 16 (over y_lo, x, core), gz: 4 (over z).
Axes of the slice: x: 4, y: 4 (y_hi: 2, y_lo: 2; y = y_hi * 2 + y_lo), z: 4, core: 2. Of those that a mesh axis runs over, the one named last changes fastest.
Arguments:
- magnetic: float32 [8, 3, 16, 256, 512], P(None, None, 'gx', 'gy', 'gz'), may hold values from -6 to 6
- velocity: float32 [3, 16, 256, 512], P(None, 'gx', 'gy', 'gz'), may hold values from -6 to 6
- shear_shift: int32 [2], replicated, may hold values from 0 to 255
- freq_index: int32 [2], replicated, may hold values from 1 to 5
Outputs:
- section_rate: float32 [8, 3, 16, 256, 512], P(None, None, 'gx', 'gy', 'gz')
- advanced: float32 [8, 3, 16, 256, 512], P(None, None, 'gx', 'gy', 'gz')
The draws below stay inside these ranges and needn't reach their ends.
Inputs may be any that keep to these rules, and one draw needn't show every extreme that they name: `shear_shift`: element 0 is the azimuthal offset of the left radial boundary, element 1 that of the right one. `freq_index`: wavenumbers in units of 2 pi / 512.
All inputs are finite; a program needn't handle non-finite values.
Results may differ from the reference program's by a relative error of at most 0.00007.
Values sent between devices are 32-bit elements; how exact they have to be, the bound alone decides.
No kernel may reach another device: no remote copies, remote signals or barrier semaphores. Data moves between devices by JAX's collectives and lax.ppermute only.
A program may use at most 128 MiB of HBM per device.

```python
import math
import jax
import jax.numpy as jnp
from jax import lax

NTEST = 8
NFREQ = 2
NX = 16
NY = 256
NZ = 512


def block_levels(rng, shape, cuts, low, top_value):
    def one(axis_at, shards_of):
        draws = jax.random.uniform(jax.random.fold_in(jax.random.fold_in(rng, 6), axis_at), (shards_of,), jnp.float32, low / len(cuts), top_value / len(cuts))
        return jnp.repeat(jnp.exp(draws), shape[axis_at] // shards_of).reshape((-1,) + (1,) * (len(shape) - axis_at - 1))

    gain = one(*cuts[0])
    for cut in cuts[1:]:
        gain = gain * one(*cut)
    return gain


def noise(key, extent, scale, bound, pieces=(), kind=jnp.bfloat16):
    factor_of = block_levels(key, extent, pieces, -0.22, 0.18) if pieces else 1.0
    drawn = jax.random.normal(key, extent, jnp.float32) * scale * factor_of
    return jnp.minimum(jnp.maximum(drawn, -bound), bound).astype(kind)


def setup_inputs(seed: int = 0) -> dict:
    key_of = jax.random.split(jax.random.key(seed), 5)
    return {
        "magnetic": noise(key_of[0], (NTEST, 3, NX, NY, NZ), 1.0, 6.0, ((2, 2), (3, 16), (4, 4)), jnp.float32),
        "velocity": noise(key_of[1], (3, NX, NY, NZ), 1.0, 6.0, ((1, 2), (2, 16), (3, 4)), jnp.float32),
        "shear_shift": jax.random.randint(key_of[2], (2,), 0, NY).astype(jnp.int32),
        "freq_index": jax.random.randint(key_of[3], (NFREQ,), 1, 6).astype(jnp.int32),
    }


SHEAR_RATE = 1.5
TIME_STEP = 0.2
DIFFUSIVITY = 0.1
SECTION_WEIGHT = 1.0 / 3.0


def test_fields(freq_index, positions, total_z):
    phase = (2.0 * math.pi) * freq_index.astype(jnp.float32)[:, None] * positions[None, :] / total_z
    cosine = jnp.cos(phase)
    sine = jnp.sin(phase)
    zeros = jnp.zeros_like(cosine)
    table = jnp.stack([jnp.stack([cosine, zeros, zeros], 1), jnp.stack([sine, zeros, zeros], 1),
                       jnp.stack([zeros, cosine, zeros], 1), jnp.stack([zeros, sine, zeros], 1)], 1)
    return table.reshape(4 * freq_index.shape[0], 3, positions.shape[0])


def motive_force(velocity, magnetic, waves):
    combined = magnetic + waves[:, :, None, None, :]
    flow_x, flow_y, flow_z = velocity[0], velocity[1], velocity[2]
    full_x, full_y, full_z = combined[:, 0], combined[:, 1], combined[:, 2]
    return jnp.stack([flow_y * full_z - flow_z * full_y, flow_z * full_x - flow_x * full_z,
                      flow_x * full_y - flow_y * full_x], 1)


def first_diff(padded, along, length):
    def window(offset_cells):
        return lax.slice_in_dim(padded, 3 + offset_cells, 3 + offset_cells + length, axis=along)
    return (45.0 * (window(1) - window(-1)) - 9.0 * (window(2) - window(-2)) + (window(3) - window(-3))) / 60.0


def second_diff(padded, along, length):
    def window(offset_cells):
        return lax.slice_in_dim(padded, 3 + offset_cells, 3 + offset_cells + length, axis=along)
    return (2.0 * (window(3) + window(-3)) - 27.0 * (window(2) + window(-2))
            + 270.0 * (window(1) + window(-1)) - 490.0 * window(0)) / 180.0


def section_rate_of(grad_x, grad_y, grad_z, laplace, magnetic, waves):
    curl_x = grad_y[:, 2] - grad_z[:, 1]
    curl_y = grad_z[:, 0] - grad_x[:, 2]
    curl_z = grad_x[:, 1] - grad_y[:, 0]
    stretch = -SHEAR_RATE * (magnetic[:, 0] + waves[:, 0, None, None, :])
    return TIME_STEP * jnp.stack([curl_x + DIFFUSIVITY * laplace[:, 0],
                                  curl_y + DIFFUSIVITY * laplace[:, 1] + stretch,
                                  curl_z + DIFFUSIVITY * laplace[:, 2]], 1)


def wrap_pad(values, along):
    length = values.shape[along]
    return jnp.concatenate([lax.slice_in_dim(values, length - 3, length, axis=along), values,
                            lax.slice_in_dim(values, 0, 3, axis=along)], axis=along)


def shear_pad(values, shear_shift):
    length = values.shape[2]
    left_ghost = jnp.roll(values[:, :, length - 3:], -shear_shift[0], axis=3)
    right_ghost = jnp.roll(values[:, :, :3], shear_shift[1], axis=3)
    return jnp.concatenate([left_ghost, values, right_ghost], axis=2)


def shear_advect(sectioned):
    spectrum = jnp.fft.rfft(sectioned, axis=3)
    modes = jnp.arange(NY // 2 + 1).astype(jnp.float32)
    sigma = -SHEAR_RATE * SECTION_WEIGHT * TIME_STEP * (jnp.arange(NX).astype(jnp.float32) + 0.5 - NX / 2.0)
    angles = (2.0 * math.pi / NY) * sigma[:, None] * modes[None, :]
    cos_phase = jnp.cos(angles)[:, :, None]
    sin_phase = jnp.sin(angles)[:, :, None]
    real_part = spectrum.real
    imag_part = spectrum.imag
    rotated = lax.complex(real_part * cos_phase + imag_part * sin_phase,
                          imag_part * cos_phase - real_part * sin_phase)
    return jnp.fft.irfft(rotated, n=NY, axis=3)


def reference(magnetic, velocity, shear_shift, freq_index):
    all_waves = test_fields(freq_index, jnp.arange(NZ).astype(jnp.float32), NZ)

    def one_problem(inputs):
        problem = inputs[0][None]
        waves = inputs[1][None]
        forcing = motive_force(velocity, problem, waves)
        grad_x = first_diff(shear_pad(forcing, shear_shift), 2, NX)
        grad_y = first_diff(wrap_pad(forcing, 3), 3, NY)
        grad_z = first_diff(wrap_pad(forcing, 4), 4, NZ)
        laplace = (second_diff(shear_pad(problem, shear_shift), 2, NX)
                   + second_diff(wrap_pad(problem, 3), 3, NY)
                   + second_diff(wrap_pad(problem, 4), 4, NZ))
        section_rates = section_rate_of(grad_x, grad_y, grad_z, laplace, problem, waves)
        moved = shear_advect(problem + SECTION_WEIGHT * section_rates)
        return section_rates[0], moved[0]

    section_rate, advanced = lax.map(one_problem, (magnetic, all_waves))
    return section_rate, advanced
```

```python
import functools
import math

import jax
import jax.numpy as jnp
import ml_dtypes
import numpy as np
from jax import lax
from jax.experimental import pallas as pl
from jax.experimental.pallas import tpu as pltpu
from jax.sharding import PartitionSpec as P

SHEAR_RATE = 1.5
TIME_STEP = 0.2
DIFFUSIVITY = 0.1
SECTION_WEIGHT = 1.0 / 3.0

D1 = [TIME_STEP * w / 60.0 for w in (45.0, -9.0, 1.0)]
D2 = [TIME_STEP * DIFFUSIVITY * w / 180.0 for w in (270.0, -27.0, 2.0)]
D2_CENTRE = -TIME_STEP * DIFFUSIVITY * 490.0 / 180.0
STRETCH = -TIME_STEP * SHEAR_RATE

BF16 = jnp.bfloat16
F32 = jnp.float32


def np_split(value):
    value = np.asarray(value, np.float64)
    high = value.astype(np.float32).astype(ml_dtypes.bfloat16)
    low = (value - high.astype(np.float64)).astype(np.float32).astype(ml_dtypes.bfloat16)
    return high, low


def stencil_1d(first_out, outs, size, centre):
    one = np.zeros((outs, size))
    two = np.zeros((outs, size))
    for row in range(outs):
        at = first_out + row
        for d in (1, 2, 3):
            if 0 <= at + d < size:
                one[row, at + d] += D1[d - 1]
                two[row, at + d] += D2[d - 1]
            if 0 <= at - d < size:
                one[row, at - d] -= D1[d - 1]
                two[row, at - d] += D2[d - 1]
        if 0 <= at < size:
            two[row, at] += centre
    return one, two


def left_weights(cx, cy):
    eye_x, eye_y = np.eye(cx), np.eye(cy)
    x1, x2 = stencil_1d(0, cx, cx, D2_CENTRE)
    y1, y2 = stencil_1d(0, cy, cy, D2_CENTRE)
    xl1, xl2 = stencil_1d(-3, 3, cx, 0.0)
    xh1, xh2 = stencil_1d(cx, 3, cx, 0.0)
    yl1, yl2 = stencil_1d(-3, 3, cy, 0.0)
    yh1, yh2 = stencil_1d(cy, 3, cy, 0.0)

    def face_y(rows):
        return np.einsum("iy,xz->ixzy", rows, eye_x).reshape(3 * cx, cx * cy)

    none_x = np.zeros((3 * cy, cx * cy))
    none_y = np.zeros((3 * cx, cx * cy))
    dx = np.concatenate([np.kron(x1, eye_y), np.kron(xl1, eye_y), np.kron(xh1, eye_y), none_y, none_y])
    dy = np.concatenate([np.kron(eye_x, y1), none_x, none_x, face_y(yl1), face_y(yh1)])
    lap = np.concatenate([
        np.kron(x2, eye_y) + np.kron(eye_x, y2),
        np.kron(xl2, eye_y), np.kron(xh2, eye_y), face_y(yl2), face_y(yh2),
    ])
    out_x = np.concatenate([dy, lap], 1)
    out_y = np.concatenate([-dx, lap], 1)
    out_z = np.concatenate([dx, -dy, lap], 1)
    result = []
    for value in (out_x, out_y, out_z):
        high, low = np_split(value)
        result.append(np.concatenate([high, high, low], 1))
    return result


def right_weights(cz):
    one, two = stencil_1d(0, cz, cz, D2_CENTRE)
    lo1, lo2 = stencil_1d(-3, 3, cz, 0.0)
    hi1, hi2 = stencil_1d(cz, 3, cz, 0.0)
    pad = np.zeros((2, cz))
    face1 = np.concatenate([lo1, hi1, pad])
    face2 = np.concatenate([lo2, hi2, pad])
    mains, faces = [], []
    for main, face in (
        (np.concatenate([-one.T, two.T]), np.concatenate([-face1, face2], 1)),
        (np.concatenate([one.T, two.T]), np.concatenate([face1, face2], 1)),
        (two.T, face2),
    ):
        high, low = np_split(main)
        mains.append(np.concatenate([high, high, low], 0))
        high, low = np_split(face)
        faces.append(np.concatenate([high, high, low], 1))
    return mains, faces


def shift_matrices(total_x, total_y):
    modes = np.arange(total_y // 2 + 1)
    sigma = -SHEAR_RATE * SECTION_WEIGHT * TIME_STEP * (np.arange(total_x) + 0.5 - total_x / 2.0)
    weight = np.full(modes.shape, 2.0)
    weight[0] = 1.0
    away = np.arange(total_y)
    rows = []
    for s in sigma:
        terms = weight[:-1, None] * np.cos(2.0 * np.pi / total_y * modes[:-1, None] * (away[None, :] - s))
        nyquist = np.cos(np.pi * s) * np.cos(np.pi * away)
        rows.append((terms.sum(0) + nyquist) / total_y)
    index = (away[:, None] - away[None, :]) % total_y
    full = np.stack(rows)[:, index]
    high, low = np_split(full)
    return np.concatenate([high, low], 2)


def split(value):
    high = value.astype(BF16)
    low = (value - high.astype(F32)).astype(BF16)
    return high, low


def rates_kernel(m_ref, v_ref, w_ref, lx_ref, ly_ref, lz_ref, rx_ref, ry_ref, rz_ref, fx_ref, fy_ref, fz_ref,
                 rate_ref, x0_ref, x1_ref, y0_ref, y1_ref, z_ref):
    problems, comps, cx, cy, cz = m_ref.shape
    cells = cx * cy
    planes = problems * comps * 3

    @pl.loop(0, problems)
    def _(p):
        m = [m_ref[p, c].reshape(cells, cz) for c in range(3)]
        v = [v_ref[c].reshape(cells, cz) for c in range(3)]
        wave = w_ref[p]
        tx = m[0] + wave[0:1]
        ty = m[1] + wave[1:2]
        tz = m[2]
        f = [
            v[1] * tz - v[2] * ty,
            v[2] * tx - v[0] * tz,
            v[0] * ty - v[1] * tx,
        ]
        fh, fl = zip(*[split(a) for a in f])
        mh, ml = zip(*[split(a) for a in m])
        lefts = (
            (lx_ref, [fh[2], mh[0], fl[2], ml[0], fh[2], mh[0]]),
            (ly_ref, [fh[2], mh[1], fl[2], ml[1], fh[2], mh[1]]),
            (lz_ref, [fh[1], fh[0], mh[2], fl[1], fl[0], ml[2], fh[1], fh[0], mh[2]]),
        )
        rights = (
            (rx_ref, fx_ref, [fh[1], mh[0], fl[1], ml[0], fh[1], mh[0]]),
            (ry_ref, fy_ref, [fh[0], mh[1], fl[0], ml[1], fh[0], mh[1]]),
            (rz_ref, fz_ref, [mh[2], ml[2], mh[2]]),
        )
        for c in range(3):
            weights, data = lefts[c]
            left = jnp.dot(weights[...], jnp.concatenate(data, 0), preferred_element_type=F32)
            main, face, data = rights[c]
            data = jnp.concatenate(data, 1)
            rate = left[:cells] + jnp.dot(data, main[...], preferred_element_type=F32)
            if c == 1:
                rate = rate + STRETCH * tx
            rate_ref[p, c] = rate.reshape(cx, cy, cz)
            z_ref[p, c] = lax.dot_general(face[...], data, (((1,), (1,)), ((), ())), preferred_element_type=F32)
            at = cells
            for ref in (x0_ref, x1_ref):
                for i in range(3):
                    ref[pl.ds(p * comps * 3 + c * 3 + i, cy, stride=planes), :] = left[at:at + cy]
                    at += cy
            for ref in (y0_ref, y1_ref):
                ref[p, c] = left[at:at + 3 * cx].reshape(3, cx, cz)
                at += 3 * cx


def finish_kernel(offset_ref, m_ref, local_ref, x0_ref, follow_ref, x1_ref, y0_ref, y1_ref, zup_ref, zdown_ref,
                  rate_ref, section_ref, joined_ref):
    problems, comps, cx, cy, cz = m_ref.shape
    cells = cx * cy
    planes = problems * comps * 3
    half = cy * planes
    joined_ref[0:half] = x0_ref[...]
    joined_ref[half:] = follow_ref[...]
    first = offset_ref[0] * planes
    rows = lax.broadcasted_iota(jnp.int32, (8, cz), 0)
    lanes = lax.broadcasted_iota(jnp.int32, (8, cz), 1)
    place = jnp.where((rows < 3) & (lanes == cz - 3 + rows), 1.0, 0.0) + jnp.where(
        (rows >= 3) & (rows < 6) & (lanes == rows - 3), 1.0, 0.0)
    zrow = lax.broadcasted_iota(jnp.int32, (8, cells), 0)

    @pl.loop(0, problems)
    def _(p):
        for c in range(3):
            ghosts = jnp.where(zrow < 3, zup_ref[p, c], zdown_ref[p, c])
            spread = lax.dot_general(ghosts, place, (((0,), (0,)), ((), ())),
                                     preferred_element_type=F32, precision=lax.Precision.HIGHEST)
            k = p * comps * 3 + c * 3
            spread = spread.reshape(cx, cy, cz)
            for x in range(cx):
                value = local_ref[p, c, x] + spread[x]
                if x < 3:
                    value = value + x1_ref[pl.ds(k + x, cy, stride=planes), :]
                if x >= cx - 3:
                    value = value + joined_ref[pl.ds(first + k + x - (cx - 3), cy, stride=planes), :]
                low = jnp.concatenate([y1_ref[p, c, i, x:x + 1] for i in range(3)], 0)
                high = jnp.concatenate([y0_ref[p, c, i, x:x + 1] for i in range(3)], 0)
                value = value + jnp.concatenate([low, jnp.zeros((cy - 6, cz), F32), high], 0)
                rate_ref[p, c, x] = value
                section_ref[x, p * comps + c] = m_ref[p, c, x] + SECTION_WEIGHT * value


def shift_kernel(data_ref, table_ref, out_ref):
    blocks, rows, cy, cz = data_ref.shape
    total = blocks * cy
    high = table_ref[:, :total]
    low = table_ref[:, total:]
    for row in range(0, rows, 2):
        data = jnp.concatenate([data_ref[:, r].reshape(total, cz) for r in (row, row + 1)], 1)
        dh, dl = split(data)
        out = (jnp.dot(high, dh, preferred_element_type=F32) + jnp.dot(high, dl, preferred_element_type=F32)
               + jnp.dot(low, dh, preferred_element_type=F32))
        out_ref[:, row] = out[:, :cz].reshape(blocks, cy, cz)
        out_ref[:, row + 1] = out[:, cz:].reshape(blocks, cy, cz)


def reorder_kernel(in_ref, out_ref):
    cx, rows = in_ref.shape[:2]
    for x in range(cx):
        out_ref[:, x] = in_ref[x]


def struct(*shape):
    return jax.ShapeDtypeStruct(shape, F32)


VMEM = pl.BlockSpec(memory_space=pltpu.VMEM)
PARAMS = pltpu.CompilerParams(vmem_limit_bytes=48 * 1024 * 1024)


def wave_table(freq_index, positions, total_z):
    phase = 2.0 * math.pi * freq_index.astype(F32)[:, None] * positions[None, :] / total_z
    cosine, sine = jnp.cos(phase), jnp.sin(phase)
    zeros = jnp.zeros_like(cosine)
    table = jnp.stack([
        jnp.stack([cosine, zeros], 1), jnp.stack([sine, zeros], 1),
        jnp.stack([zeros, cosine], 1), jnp.stack([zeros, sine], 1),
    ], 1)
    return table.reshape(4 * freq_index.shape[0], 2, positions.shape[0])


def on_device(magnetic, velocity, shear_shift, freq_index):
    problems, comps, cx, cy, cz = magnetic.shape
    nx, ny, nz = lax.axis_size("gx"), lax.axis_size("gy"), lax.axis_size("gz")
    total_x, total_y, total_z = cx * nx, cy * ny, cz * nz
    gx, gy, gz = lax.axis_index("gx"), lax.axis_index("gy"), lax.axis_index("gz")
    positions = (gz * cz + jnp.arange(cz)).astype(F32)
    waves = wave_table(freq_index, positions, total_z)
    lefts = [jnp.asarray(w) for w in left_weights(cx, cy)]
    mains, faces = right_weights(cz)
    mains, faces = [jnp.asarray(w) for w in mains], [jnp.asarray(w) for w in faces]
    planes = problems * comps * 3
    local, x0, x1, y0, y1, z = pl.pallas_call(
        rates_kernel,
        out_shape=(
            struct(problems, comps, cx, cy, cz), struct(cy * planes, cz), struct(cy * planes, cz),
            struct(problems, comps, 3, cx, cz), struct(problems, comps, 3, cx, cz),
            struct(problems, comps, 8, cx * cy),
        ),
        in_specs=[VMEM] * 12, out_specs=(VMEM,) * 6, compiler_params=PARAMS,
    )(magnetic, velocity, waves, *lefts, *mains, *faces)

    def at(x, y):
        return (x % nx) * ny + y % ny

    down = [(j, (j - 1) % ny) for j in range(ny)]
    up = [(j, (j + 1) % ny) for j in range(ny)]
    zdown = [(j, (j - 1) % nz) for j in range(nz)]
    zup = [(j, (j + 1) % nz) for j in range(nz)]
    follow = [(at(1, j + 1), at(1, j)) for j in range(ny)]
    low_amount = (total_y - shear_shift[1]) % total_y
    high_amount = shear_shift[0]

    def towards_low(q):
        return [(at(0, j + q), at(1, j)) for j in range(ny)] + [(at(1, j), at(0, j)) for j in range(ny)]

    def towards_high(q):
        return [(at(1, j + q), at(0, j)) for j in range(ny)] + [(at(0, j), at(1, j)) for j in range(ny)]

    def routed(value, route, q):
        return lax.switch(q, [functools.partial(lax.ppermute, axis_name=("gx", "gy"), perm=route(i)) for i in range(ny)],
                          value)

    x1_next = lax.ppermute(x1, ("gx", "gy"), follow)
    y0_in = lax.ppermute(y0, "gy", down)
    y1_in = lax.ppermute(y1, "gy", up)
    z_up = lax.ppermute(z, "gz", zdown)
    z_down = lax.ppermute(z, "gz", zup)
    x0_in = routed(x0, towards_low, low_amount // cy)
    x0_next = lax.ppermute(x0_in, ("gx", "gy"), follow)
    start = jnp.where(gx == 1, high_amount % cy, 0)
    x1_rows = lax.dynamic_slice_in_dim(
        jnp.concatenate([x1.reshape(cy, planes, cz), x1_next.reshape(cy, planes, cz)], 0), start, cy, 0)
    x1_in = routed(x1_rows.reshape(cy * planes, cz), towards_high, high_amount // cy)
    offset = jnp.where(gx == 1, low_amount % cy, 0).astype(jnp.int32).reshape(1)
    rate, section = pl.pallas_call(
        finish_kernel,
        out_shape=(struct(problems, comps, cx, cy, cz), struct(cx, problems * comps, cy, cz)),
        in_specs=[pl.BlockSpec(memory_space=pltpu.SMEM)] + [VMEM] * 9, out_specs=(VMEM,) * 2,
        scratch_shapes=[pltpu.VMEM((2 * cy * planes, cz), F32)],
        compiler_params=PARAMS,
    )(offset, magnetic, local, x0_in, x0_next, x1_in, y0_in, y1_in, z_up, z_down)

    rows = cx * problems * comps
    tables = jnp.asarray(shift_matrices(total_x, total_y))
    table = lax.dynamic_index_in_dim(tables, gx * cx + gy * (rows // ny) // (problems * comps), 0, keepdims=False)
    pencil = lax.all_to_all(section.reshape(rows, cy, cz), "gy", 0, 0, tiled=True)
    turned = pl.pallas_call(
        shift_kernel, out_shape=struct(ny, rows // ny, cy, cz), in_specs=[VMEM] * 2, out_specs=VMEM,
        compiler_params=PARAMS,
    )(pencil.reshape(ny, rows // ny, cy, cz), table)
    returned = lax.all_to_all(turned.reshape(rows, cy, cz), "gy", 0, 0, tiled=True)
    advanced = pl.pallas_call(
        reorder_kernel, out_shape=struct(problems * comps, cx, cy, cz), in_specs=[VMEM], out_specs=VMEM,
        compiler_params=PARAMS,
    )(returned.reshape(cx, problems * comps, cy, cz))
    return rate, advanced.reshape(magnetic.shape)


def solution(mesh):
    return jax.shard_map(
        on_device,
        mesh=mesh,
        in_specs=(P(None, None, "gx", "gy", "gz"), P(None, "gx", "gy", "gz"), P(), P()),
        out_specs=(P(None, None, "gx", "gy", "gz"), P(None, None, "gx", "gy", "gz")),
        check_vma=False,
    )
```

```python
import functools
import math

import jax
import jax.numpy as jnp
import ml_dtypes
import numpy as np
from jax import lax
from jax.experimental import pallas as pl
from jax.experimental.pallas import tpu as pltpu
from jax.sharding import PartitionSpec as P

SHEAR_RATE = 1.5
TIME_STEP = 0.2
DIFFUSIVITY = 0.1
SECTION_WEIGHT = 1.0 / 3.0

D1 = [TIME_STEP * w / 60.0 for w in (45.0, -9.0, 1.0)]
D2 = [TIME_STEP * DIFFUSIVITY * w / 180.0 for w in (270.0, -27.0, 2.0)]
D2_CENTRE = -TIME_STEP * DIFFUSIVITY * 490.0 / 180.0
STRETCH = -TIME_STEP * SHEAR_RATE

BF16 = jnp.bfloat16
F32 = jnp.float32


def np_split(value):
    value = np.asarray(value, np.float64)
    high = value.astype(np.float32).astype(ml_dtypes.bfloat16)
    low = (value - high.astype(np.float64)).astype(np.float32).astype(ml_dtypes.bfloat16)
    return high, low


def stencil_1d(first_out, outs, size, centre):
    one = np.zeros((outs, size))
    two = np.zeros((outs, size))
    for row in range(outs):
        at = first_out + row
        for d in (1, 2, 3):
            if 0 <= at + d < size:
                one[row, at + d] += D1[d - 1]
                two[row, at + d] += D2[d - 1]
            if 0 <= at - d < size:
                one[row, at - d] -= D1[d - 1]
                two[row, at - d] += D2[d - 1]
        if 0 <= at < size:
            two[row, at] += centre
    return one, two


def left_weights(cx, cy):
    eye_x, eye_y = np.eye(cx), np.eye(cy)
    x1, x2 = stencil_1d(0, cx, cx, D2_CENTRE)
    y1, y2 = stencil_1d(0, cy, cy, D2_CENTRE)
    xl1, xl2 = stencil_1d(-3, 3, cx, 0.0)
    xh1, xh2 = stencil_1d(cx, 3, cx, 0.0)
    yl1, yl2 = stencil_1d(-3, 3, cy, 0.0)
    yh1, yh2 = stencil_1d(cy, 3, cy, 0.0)

    def face_y(rows):
        return np.einsum("iy,xz->ixzy", rows, eye_x).reshape(3 * cx, cx * cy)

    none_x = np.zeros((3 * cy, cx * cy))
    none_y = np.zeros((3 * cx, cx * cy))
    dx = np.concatenate([np.kron(x1, eye_y), np.kron(xl1, eye_y), np.kron(xh1, eye_y), none_y, none_y])
    dy = np.concatenate([np.kron(eye_x, y1), none_x, none_x, face_y(yl1), face_y(yh1)])
    lap = np.concatenate([
        np.kron(x2, eye_y) + np.kron(eye_x, y2),
        np.kron(xl2, eye_y), np.kron(xh2, eye_y), face_y(yl2), face_y(yh2),
    ])
    out_x = np.concatenate([dy, lap], 1)
    out_y = np.concatenate([-dx, lap], 1)
    out_z = np.concatenate([dx, -dy, lap], 1)
    result = []
    for value in (out_x, out_y, out_z):
        high, low = np_split(value)
        result.append(np.concatenate([high, high, low], 1))
    return result


def right_weights(cz):
    one, two = stencil_1d(0, cz, cz, D2_CENTRE)
    lo1, lo2 = stencil_1d(-3, 3, cz, 0.0)
    hi1, hi2 = stencil_1d(cz, 3, cz, 0.0)
    pad = np.zeros((2, cz))
    face1 = np.concatenate([lo1, hi1, pad])
    face2 = np.concatenate([lo2, hi2, pad])
    mains, faces = [], []
    for main, face in (
        (np.concatenate([-one.T, two.T]), np.concatenate([-face1, face2], 1)),
        (np.concatenate([one.T, two.T]), np.concatenate([face1, face2], 1)),
        (two.T, face2),
    ):
        high, low = np_split(main)
        mains.append(np.concatenate([high, high, low], 0))
        high, low = np_split(face)
        faces.append(np.concatenate([high, high, low], 1))
    return mains, faces


def shift_matrices(total_x, total_y):
    modes = np.arange(total_y // 2 + 1)
    sigma = -SHEAR_RATE * SECTION_WEIGHT * TIME_STEP * (np.arange(total_x) + 0.5 - total_x / 2.0)
    weight = np.full(modes.shape, 2.0)
    weight[0] = 1.0
    away = np.arange(total_y)
    rows = []
    for s in sigma:
        terms = weight[:-1, None] * np.cos(2.0 * np.pi / total_y * modes[:-1, None] * (away[None, :] - s))
        nyquist = np.cos(np.pi * s) * np.cos(np.pi * away)
        rows.append((terms.sum(0) + nyquist) / total_y)
    index = (away[:, None] - away[None, :]) % total_y
    full = np.stack(rows)[:, index]
    high, low = np_split(full)
    return np.concatenate([high, low], 2)


def split(value):
    high = value.astype(BF16)
    low = (value - high.astype(F32)).astype(BF16)
    return high, low


def rates_kernel(freq_ref, shift_ref, m_ref, v_ref, lx_ref, ly_ref, lz_ref, rx_ref, ry_ref, rz_ref, fx_ref, fy_ref, fz_ref,
                 rate_ref, x0_ref, x1_ref, y0_ref, y1_ref, z_ref, low_ref, high_ref, *, total_y, total_z):
    pair, comps, cx, cy, cz = m_ref.shape
    low_ref[0] = ((total_y - shift_ref[1]) & (total_y - 1)) // cy
    high_ref[0] = shift_ref[0] // cy
    cells = cx * cy
    planes = x0_ref.shape[0] // cy
    p = pl.program_id(0) * pair

    def wide(parts):
        return jnp.concatenate(parts, 1)

    def tall(value):
        return jnp.concatenate([value[:, i * cz:(i + 1) * cz] for i in range(pair)], 0)

    m = [wide([m_ref[i, c].reshape(cells, cz) for i in range(pair)]) for c in range(3)]
    v = [wide([v_ref[c].reshape(cells, cz)] * pair) for c in range(3)]
    step = pl.program_id(0)
    position = (lax.axis_index("gz") * cz + lax.broadcasted_iota(jnp.int32, (1, cz), 1)).astype(F32)
    phase = 2.0 * math.pi * freq_ref[step // 2].astype(F32) * position / total_z
    wave = wide([jnp.cos(phase), jnp.sin(phase)])
    along_x = step % 2 == 0
    tx = m[0] + jnp.where(along_x, wave, 0.0)
    ty = m[1] + jnp.where(along_x, 0.0, wave)
    tz = m[2]
    f = [
        v[1] * tz - v[2] * ty,
        v[2] * tx - v[0] * tz,
        v[0] * ty - v[1] * tx,
    ]
    fh, fl = zip(*[split(a) for a in f])
    mh, ml = zip(*[split(a) for a in m])
    lefts = (
        (lx_ref, [fh[2], mh[0], fl[2], ml[0], fh[2], mh[0]]),
        (ly_ref, [fh[2], mh[1], fl[2], ml[1], fh[2], mh[1]]),
        (lz_ref, [fh[1], fh[0], mh[2], fl[1], fl[0], ml[2], fh[1], fh[0], mh[2]]),
    )
    rights = (
        (rx_ref, fx_ref, [fh[1], mh[0], fl[1], ml[0], fh[1], mh[0]]),
        (ry_ref, fy_ref, [fh[0], mh[1], fl[0], ml[1], fh[0], mh[1]]),
        (rz_ref, fz_ref, [mh[2], ml[2], mh[2]]),
    )
    for c in range(3):
        weights, data = lefts[c]
        left = jnp.dot(weights[...], jnp.concatenate(data, 0), preferred_element_type=F32)
        if c == 1:
            main_left = left[:cells] + STRETCH * tx
        else:
            main_left = left[:cells]
        main, face, data = rights[c]
        data = jnp.concatenate([tall(d) for d in data], 1)
        right = jnp.dot(data, main[...], preferred_element_type=F32)
        ghost = lax.dot_general(face[...], data, (((1,), (1,)), ((), ())), preferred_element_type=F32)
        for i in range(pair):
            lanes = slice(i * cz, (i + 1) * cz)
            rate = main_left[:, lanes] + right[i * cells:(i + 1) * cells]
            rate_ref[i, c] = rate.reshape(cx, cy, cz)
            z_ref[i, c] = ghost[:, i * cells:(i + 1) * cells]
            at = cells
            for ref in (x0_ref, x1_ref):
                for j in range(3):
                    ref[pl.ds((p + i) * comps * 3 + c * 3 + j, cy, stride=planes), :] = left[at:at + cy, lanes]
                    at += cy
            for ref in (y0_ref, y1_ref):
                ref[i, c] = left[at:at + 3 * cx, lanes].reshape(3, cx, cz)
                at += 3 * cx


def three(value):
    high = value.astype(BF16)
    rest = value - high.astype(F32)
    middle = rest.astype(BF16)
    return [high, middle, (rest - middle.astype(F32)).astype(BF16)]


def place_weights(cx, cy, cz, comps):
    left = np.zeros((cx * cy, 6 * cx))
    for i in range(3):
        for x in range(cx):
            left[x * cy + i, i * cx + x] = 1.0
            left[x * cy + cy - 3 + i, 3 * cx + i * cx + x] = 1.0
    right = np.zeros((8 * comps, comps * cz))
    for c in range(comps):
        for i in range(3):
            right[8 * c + i, c * cz + cz - 3 + i] = 1.0
            right[8 * c + 3 + i, c * cz + i] = 1.0
    return (np.concatenate([left] * 3, 1).astype(ml_dtypes.bfloat16),
            np.concatenate([right] * 3, 0).astype(ml_dtypes.bfloat16))


def finish_kernel(shift_ref, m_ref, local_ref, x0_ref, follow_ref, x1_ref, y0_ref, y1_ref, zup_ref, zdown_ref,
                  left_ref, right_ref, rate_ref, section_ref, joined_ref):
    pair, comps, cx, cy, cz = m_ref.shape
    cells = cx * cy
    half = x0_ref.shape[0]
    planes = half // cy
    step = pl.program_id(0)

    @pl.when(step == 0)
    def _():
        joined_ref[0:half] = x0_ref[...]
        joined_ref[half:] = follow_ref[...]

    first = jnp.where(lax.axis_index("gx") == 1, (cy - (shift_ref[1] & (cy - 1))) & (cy - 1), 0) * planes
    zrow = lax.broadcasted_iota(jnp.int32, (8, cells), 0)
    for i in range(pair):
        ghosts = jnp.concatenate([jnp.where(zrow < 3, zup_ref[i, c], zdown_ref[i, c]) for c in range(comps)], 0)
        ghosts = jnp.concatenate(three(ghosts), 0)
        faces = jnp.concatenate([
            jnp.concatenate([y1_ref[i, c].reshape(3 * cx, cz), y0_ref[i, c].reshape(3 * cx, cz)], 0)
            for c in range(comps)], 1)
        placed = jnp.dot(left_ref[...], jnp.concatenate(three(faces), 0), preferred_element_type=F32)
        placed = placed + lax.dot_general(ghosts, right_ref[...], (((0,), (0,)), ((), ())), preferred_element_type=F32)
        for c in range(comps):
            k = (step * pair + i) * comps * 3 + c * 3
            spread = placed[:, c * cz:(c + 1) * cz].reshape(cx, cy, cz)
            for x in range(cx):
                value = local_ref[i, c, x] + spread[x]
                if x < 3:
                    value = value + x1_ref[pl.ds(k + x, cy, stride=planes), :]
                if x >= cx - 3:
                    value = value + joined_ref[pl.ds(first + k + x - (cx - 3), cy, stride=planes), :]
                rate_ref[i, c, x] = value
                section_ref[x, i * comps + c] = m_ref[i, c, x] + SECTION_WEIGHT * value


def shift_kernel(data_ref, table_ref, out_ref):
    blocks, rows, cy, cz = data_ref.shape
    total = blocks * cy
    high = table_ref[:, :total]
    low = table_ref[:, total:]
    for row in range(0, rows, 2):
        data = jnp.concatenate([data_ref[:, r].reshape(total, cz) for r in (row, row + 1)], 1)
        dh, dl = split(data)
        out = (jnp.dot(high, dh, preferred_element_type=F32) + jnp.dot(high, dl, preferred_element_type=F32)
               + jnp.dot(low, dh, preferred_element_type=F32))
        out_ref[:, row] = out[:, :cz].reshape(blocks, cy, cz)
        out_ref[:, row + 1] = out[:, cz:].reshape(blocks, cy, cz)


def reorder_kernel(in_ref, out_ref):
    cx, rows = in_ref.shape[:2]
    for x in range(cx):
        out_ref[:, x] = in_ref[x]


def struct(*shape):
    return jax.ShapeDtypeStruct(shape, F32)


VMEM = pl.BlockSpec(memory_space=pltpu.VMEM)
SMEM = pl.BlockSpec(memory_space=pltpu.SMEM)
PARAMS = pltpu.CompilerParams(vmem_limit_bytes=40 * 1024 * 1024)
STREAMED = pltpu.CompilerParams(vmem_limit_bytes=60 * 1024 * 1024)


def on_device(magnetic, velocity, shear_shift, freq_index):
    problems, comps, cx, cy, cz = magnetic.shape
    nx, ny, nz = lax.axis_size("gx"), lax.axis_size("gy"), lax.axis_size("gz")
    total_x, total_y, total_z = cx * nx, cy * ny, cz * nz
    gx, gy = lax.axis_index("gx"), lax.axis_index("gy")
    lefts = [jnp.asarray(w) for w in left_weights(cx, cy)]
    mains, faces = right_weights(cz)
    mains, faces = [jnp.asarray(w) for w in mains], [jnp.asarray(w) for w in faces]
    planes = problems * comps * 3
    pair = 2
    steps = problems // pair

    def whole(array):
        return pl.BlockSpec(array.shape, lambda i: (0,) * len(array.shape))

    def cut(*shape):
        return pl.BlockSpec((pair,) + shape, lambda i: (i,) + (0,) * len(shape))

    tile, edge, side = (comps, cx, cy, cz), (comps, 3, cx, cz), (comps, 8, cx * cy)
    faces_x = struct(cy * planes, cz)
    weights = [*lefts, *mains, *faces]
    index = jax.ShapeDtypeStruct((1,), jnp.int32)
    local, x0, x1, y0, y1, z, low_step, high_step = pl.pallas_call(
        functools.partial(rates_kernel, total_y=total_y, total_z=total_z),
        grid=(steps,),
        out_shape=(struct(problems, *tile), faces_x, faces_x, struct(problems, *edge), struct(problems, *edge),
                   struct(problems, *side), index, index),
        in_specs=[SMEM, SMEM, cut(*tile), whole(velocity)] + [whole(w) for w in weights],
        out_specs=(cut(*tile), whole(faces_x), whole(faces_x), cut(*edge), cut(*edge), cut(*side), SMEM, SMEM),
        compiler_params=STREAMED,
    )(freq_index, shear_shift, magnetic, velocity, *weights)

    def at(x, y):
        return (x % nx) * ny + y % ny

    down = [(j, (j - 1) % ny) for j in range(ny)]
    up = [(j, (j + 1) % ny) for j in range(ny)]
    zdown = [(j, (j - 1) % nz) for j in range(nz)]
    zup = [(j, (j + 1) % nz) for j in range(nz)]
    follow = [(at(1, j + 1), at(1, j)) for j in range(ny)]
    def towards_low(q):
        return [(at(0, j + q), at(1, j)) for j in range(ny)] + [(at(1, j), at(0, j)) for j in range(ny)]

    def towards_high(q):
        return [(at(1, j + q), at(0, j)) for j in range(ny)] + [(at(0, j), at(1, j)) for j in range(ny)]

    def routed(q, route, value):
        return lax.switch(q, [functools.partial(lax.ppermute, axis_name=("gx", "gy"), perm=route(i)) for i in range(ny)],
                          value)

    beside = (lax.ppermute(x1, ("gx", "gy"), follow), lax.ppermute(y0, "gy", down), lax.ppermute(y1, "gy", up),
              lax.ppermute(z, "gz", zdown), lax.ppermute(z, "gz", zup))
    x0_in = routed(low_step[0], towards_low, x0)
    x0_in, x1_next, y0_in, y1_in, z_up, z_down = lax.optimization_barrier((x0_in, *beside))
    x0_next = lax.ppermute(x0_in, ("gx", "gy"), follow)
    start = jnp.where(gx == 1, shear_shift[0] & (cy - 1), 0)
    x1_rows = lax.dynamic_slice_in_dim(
        jnp.concatenate([x1.reshape(cy, planes, cz), x1_next.reshape(cy, planes, cz)], 0), start, cy, 0)
    x1_in = routed(high_step[0], towards_high, x1_rows.reshape(cy * planes, cz))
    placing = [jnp.asarray(w) for w in place_weights(cx, cy, cz, comps)]
    rate, section = pl.pallas_call(
        finish_kernel,
        grid=(steps,),
        out_shape=(struct(problems, *tile), struct(cx, problems * comps, cy, cz)),
        in_specs=[SMEM, cut(*tile), cut(*tile)] + [whole(faces_x)] * 3
        + [cut(*edge)] * 2 + [cut(*side)] * 2 + [whole(w) for w in placing],
        out_specs=(cut(*tile), pl.BlockSpec((cx, pair * comps, cy, cz), lambda i: (0, i, 0, 0))),
        scratch_shapes=[pltpu.VMEM((2 * cy * planes, cz), F32)],
        compiler_params=STREAMED,
    )(shear_shift, magnetic, local, x0_in, x0_next, x1_in, y0_in, y1_in, z_up, z_down, *placing)

    rows = cx * problems * comps
    tables = jnp.asarray(shift_matrices(total_x, total_y))
    table = lax.dynamic_index_in_dim(tables, gx * cx + gy * (rows // ny) // (problems * comps), 0, keepdims=False)
    pencil = lax.all_to_all(section.reshape(rows, cy, cz), "gy", 0, 0, tiled=True)
    turned = pl.pallas_call(
        shift_kernel, out_shape=struct(ny, rows // ny, cy, cz), in_specs=[VMEM] * 2, out_specs=VMEM,
        compiler_params=PARAMS,
    )(pencil.reshape(ny, rows // ny, cy, cz), table)
    returned = lax.all_to_all(turned.reshape(rows, cy, cz), "gy", 0, 0, tiled=True)
    advanced = pl.pallas_call(
        reorder_kernel, out_shape=struct(problems * comps, cx, cy, cz), in_specs=[VMEM], out_specs=VMEM,
        compiler_params=PARAMS,
    )(returned.reshape(cx, problems * comps, cy, cz))
    return rate, advanced.reshape(magnetic.shape)


def solution(mesh):
    return jax.shard_map(
        on_device,
        mesh=mesh,
        in_specs=(P(None, None, "gx", "gy", "gz"), P(None, "gx", "gy", "gz"), P(), P()),
        out_specs=(P(None, None, "gx", "gy", "gz"), P(None, None, "gx", "gy", "gz")),
        check_vma=False,
    )
```

```python
import functools
import math

import jax
import jax.numpy as jnp
import ml_dtypes
import numpy as np
from jax import lax
from jax.experimental import pallas as pl
from jax.experimental.pallas import tpu as pltpu
from jax.sharding import PartitionSpec as P

SHEAR_RATE = 1.5
TIME_STEP = 0.2
DIFFUSIVITY = 0.1
SECTION_WEIGHT = 1.0 / 3.0

D1 = [TIME_STEP * w / 60.0 for w in (45.0, -9.0, 1.0)]
D2 = [TIME_STEP * DIFFUSIVITY * w / 180.0 for w in (270.0, -27.0, 2.0)]
D2_CENTRE = -TIME_STEP * DIFFUSIVITY * 490.0 / 180.0
STRETCH = -TIME_STEP * SHEAR_RATE

BF16 = jnp.bfloat16
F32 = jnp.float32


def np_split(value):
    value = np.asarray(value, np.float64)
    high = value.astype(np.float32).astype(ml_dtypes.bfloat16)
    low = (value - high.astype(np.float64)).astype(np.float32).astype(ml_dtypes.bfloat16)
    return high, low


def stencil_1d(first_out, outs, size, centre):
    one = np.zeros((outs, size))
    two = np.zeros((outs, size))
    for row in range(outs):
        at = first_out + row
        for d in (1, 2, 3):
            if 0 <= at + d < size:
                one[row, at + d] += D1[d - 1]
                two[row, at + d] += D2[d - 1]
            if 0 <= at - d < size:
                one[row, at - d] -= D1[d - 1]
                two[row, at - d] += D2[d - 1]
        if 0 <= at < size:
            two[row, at] += centre
    return one, two


def left_weights(cx, cy):
    eye_x, eye_y = np.eye(cx), np.eye(cy)
    x1, x2 = stencil_1d(0, cx, cx, D2_CENTRE)
    y1, y2 = stencil_1d(0, cy, cy, D2_CENTRE)
    xl1, xl2 = stencil_1d(-3, 3, cx, 0.0)
    xh1, xh2 = stencil_1d(cx, 3, cx, 0.0)
    yl1, yl2 = stencil_1d(-3, 3, cy, 0.0)
    yh1, yh2 = stencil_1d(cy, 3, cy, 0.0)

    def face_y(rows):
        return np.einsum("iy,xz->ixzy", rows, eye_x).reshape(3 * cx, cx * cy)

    none_x = np.zeros((3 * cy, cx * cy))
    none_y = np.zeros((3 * cx, cx * cy))
    dx = np.concatenate([np.kron(x1, eye_y), np.kron(xl1, eye_y), np.kron(xh1, eye_y), none_y, none_y])
    dy = np.concatenate([np.kron(eye_x, y1), none_x, none_x, face_y(yl1), face_y(yh1)])
    lap = np.concatenate([
        np.kron(x2, eye_y) + np.kron(eye_x, y2),
        np.kron(xl2, eye_y), np.kron(xh2, eye_y), face_y(yl2), face_y(yh2),
    ])
    out_x = np.concatenate([dy, lap], 1)
    out_y = np.concatenate([-dx, lap], 1)
    out_z = np.concatenate([dx, -dy, lap], 1)
    result = []
    for value in (out_x, out_y, out_z):
        high, low = np_split(value)
        result.append(np.concatenate([high, high, low], 1))
    return result


def right_weights(cz):
    one, two = stencil_1d(0, cz, cz, D2_CENTRE)
    lo1, lo2 = stencil_1d(-3, 3, cz, 0.0)
    hi1, hi2 = stencil_1d(cz, 3, cz, 0.0)
    pad = np.zeros((2, cz))
    face1 = np.concatenate([lo1, hi1, pad])
    face2 = np.concatenate([lo2, hi2, pad])
    mains, faces = [], []
    for main, face in (
        (np.concatenate([-one.T, two.T]), np.concatenate([-face1, face2], 1)),
        (np.concatenate([one.T, two.T]), np.concatenate([face1, face2], 1)),
        (two.T, face2),
    ):
        high, low = np_split(main)
        mains.append(np.concatenate([high, high, low], 0))
        high, low = np_split(face)
        faces.append(np.concatenate([high, high, low], 1))
    return mains, faces


def shift_matrices(total_x, total_y):
    modes = np.arange(total_y // 2 + 1)
    sigma = -SHEAR_RATE * SECTION_WEIGHT * TIME_STEP * (np.arange(total_x) + 0.5 - total_x / 2.0)
    weight = np.full(modes.shape, 2.0)
    weight[0] = 1.0
    away = np.arange(total_y)
    rows = []
    for s in sigma:
        terms = weight[:-1, None] * np.cos(2.0 * np.pi / total_y * modes[:-1, None] * (away[None, :] - s))
        nyquist = np.cos(np.pi * s) * np.cos(np.pi * away)
        rows.append((terms.sum(0) + nyquist) / total_y)
    index = (away[:, None] - away[None, :]) % total_y
    full = np.stack(rows)[:, index]
    high, low = np_split(full)
    return np.concatenate([high, low], 2)


def split(value):
    high = value.astype(BF16)
    low = (value - high.astype(F32)).astype(BF16)
    return high, low


def rates_kernel(freq_ref, m_ref, v_ref, lx_ref, ly_ref, lz_ref, rx_ref, ry_ref, rz_ref, fx_ref, fy_ref, fz_ref,
                 rate_ref, facing_ref, outer_ref, y0_ref, y1_ref, z_ref, *, total_z):
    pair, comps, cx, cy, cz = m_ref.shape
    cells = cx * cy
    side = 3 * cy
    on_left = lax.axis_index("gx") == 0

    def wide(parts):
        return jnp.concatenate(parts, 1)

    def tall(value):
        return jnp.concatenate([value[:, i * cz:(i + 1) * cz] for i in range(pair)], 0)

    m = [wide([m_ref[i, c].reshape(cells, cz) for i in range(pair)]) for c in range(3)]
    v = [wide([v_ref[c].reshape(cells, cz)] * pair) for c in range(3)]
    step = pl.program_id(0)
    position = (lax.axis_index("gz") * cz + lax.broadcasted_iota(jnp.int32, (1, cz), 1)).astype(F32)
    phase = 2.0 * math.pi * freq_ref[step // 2].astype(F32) * position / total_z
    wave = wide([jnp.cos(phase), jnp.sin(phase)])
    along_x = step % 2 == 0
    tx = m[0] + jnp.where(along_x, wave, 0.0)
    ty = m[1] + jnp.where(along_x, 0.0, wave)
    tz = m[2]
    f = [
        v[1] * tz - v[2] * ty,
        v[2] * tx - v[0] * tz,
        v[0] * ty - v[1] * tx,
    ]
    fh, fl = zip(*[split(a) for a in f])
    mh, ml = zip(*[split(a) for a in m])
    lefts = (
        (lx_ref, [fh[2], mh[0], fl[2], ml[0], fh[2], mh[0]]),
        (ly_ref, [fh[2], mh[1], fl[2], ml[1], fh[2], mh[1]]),
        (lz_ref, [fh[1], fh[0], mh[2], fl[1], fl[0], ml[2], fh[1], fh[0], mh[2]]),
    )
    rights = (
        (rx_ref, fx_ref, [fh[1], mh[0], fl[1], ml[0], fh[1], mh[0]]),
        (ry_ref, fy_ref, [fh[0], mh[1], fl[0], ml[1], fh[0], mh[1]]),
        (rz_ref, fz_ref, [mh[2], ml[2], mh[2]]),
    )
    for c in range(3):
        weights, data = lefts[c]
        left = jnp.dot(weights[...], jnp.concatenate(data, 0), preferred_element_type=F32)
        if c == 1:
            main_left = left[:cells] + STRETCH * tx
        else:
            main_left = left[:cells]
        main, face, data = rights[c]
        data = jnp.concatenate([tall(d) for d in data], 1)
        right = jnp.dot(data, main[...], preferred_element_type=F32)
        ghost = lax.dot_general(face[...], data, (((1,), (1,)), ((), ())), preferred_element_type=F32)
        for i in range(pair):
            lanes = slice(i * cz, (i + 1) * cz)
            rate = main_left[:, lanes] + right[i * cells:(i + 1) * cells]
            rate_ref[i, c] = rate.reshape(cx, cy, cz)
            z_ref[i, c] = ghost[:, i * cells:(i + 1) * cells]
            low = left[cells:cells + side, lanes].reshape(3, cy, cz)
            high = left[cells + side:cells + 2 * side, lanes].reshape(3, cy, cz)
            facing_ref[i, c] = jnp.where(on_left, high, low)
            outer_ref[i, c] = jnp.where(on_left, low, high)
            at = cells + 2 * side
            for ref in (y0_ref, y1_ref):
                ref[i, c] = left[at:at + 3 * cx, lanes].reshape(3, cx, cz)
                at += 3 * cx


def three(value):
    high = value.astype(BF16)
    rest = value - high.astype(F32)
    middle = rest.astype(BF16)
    return [high, middle, (rest - middle.astype(F32)).astype(BF16)]


def place_weights(cx, cy, cz, comps):
    left = np.zeros((cx * cy, 6 * cx))
    for i in range(3):
        for x in range(cx):
            left[x * cy + i, i * cx + x] = 1.0
            left[x * cy + cy - 3 + i, 3 * cx + i * cx + x] = 1.0
    right = np.zeros((8 * comps, comps * cz))
    for c in range(comps):
        for i in range(3):
            right[8 * c + i, c * cz + cz - 3 + i] = 1.0
            right[8 * c + 3 + i, c * cz + i] = 1.0
    return (np.concatenate([left] * 3, 1).astype(ml_dtypes.bfloat16),
            np.concatenate([right] * 3, 0).astype(ml_dtypes.bfloat16))


FIRST = ((0, 1, 2, 6), (5, 6, 7, 3))
SECOND = ((3, 4, 5, 7), (0, 1, 2, 4))


def plane_slot(x, on_left):
    where = []
    for half in range(2):
        if x in FIRST[half]:
            where.append((FIRST[half].index(x), 0))
        else:
            where.append((SECOND[half].index(x), 3))
    return tuple(jnp.where(on_left, a, b) for a, b in zip(*where))


def finish_kernel(m_ref, local_ref, facing_ref, outer_ref, y0_ref, y1_ref, zup_ref, zdown_ref, left_ref, right_ref,
                  rate_ref, lines_ref):
    pair, comps, cx, cy, cz = m_ref.shape
    cells = cx * cy
    on_left = lax.axis_index("gx") == 0
    zrow = lax.broadcasted_iota(jnp.int32, (8, cells), 0)
    for i in range(pair):
        ghosts = jnp.concatenate([jnp.where(zrow < 3, zup_ref[i, c], zdown_ref[i, c]) for c in range(comps)], 0)
        ghosts = jnp.concatenate(three(ghosts), 0)
        faces = jnp.concatenate([
            jnp.concatenate([y1_ref[i, c].reshape(3 * cx, cz), y0_ref[i, c].reshape(3 * cx, cz)], 0)
            for c in range(comps)], 1)
        placed = jnp.dot(left_ref[...], jnp.concatenate(three(faces), 0), preferred_element_type=F32)
        placed = placed + lax.dot_general(ghosts, right_ref[...], (((0,), (0,)), ((), ())), preferred_element_type=F32)
        for c in range(comps):
            spread = placed[:, c * cz:(c + 1) * cz].reshape(cx, cy, cz)
            for x in range(cx):
                value = local_ref[i, c, x] + spread[x]
                if x < 3:
                    value = value + jnp.where(on_left, 0.0, facing_ref[i, c, x])
                if x >= cx - 3:
                    value = value + jnp.where(on_left, facing_ref[i, c, x - (cx - 3)], 0.0)
                rate_ref[i, c, x] = value
                k, row = plane_slot(x, on_left)
                lines_ref[k, i, row + c] = m_ref[i, c, x] + SECTION_WEIGHT * value
            for j in range(3):
                lines_ref[j, i, 6 + c] = outer_ref[i, c, j]
            lines_ref[3, i, 6 + c] = jnp.zeros((cy, cz), F32)


def shift_kernel(shift_ref, data_ref, table_ref, out_ref, twice_ref):
    halves, blocks, rows, cy, cz = data_ref.shape
    total = blocks * cy
    for half in range(halves):
        first = shift_ref[0] if half == 0 else (total - shift_ref[1]) & (total - 1)
        rolled = []
        for c in range(3):
            sums = data_ref[1 - half, :, 6 + c].reshape(total, cz)
            twice_ref[0:total] = sums
            twice_ref[total:2 * total] = sums
            moved = twice_ref[pl.ds(first, total), :]
            out_ref[half, :, 6 + c] = moved.reshape(blocks, cy, cz)
            rolled.append(moved)
        for group in range(2):
            data = [data_ref[half, :, 3 * group + c].reshape(total, cz) for c in range(3)]
            if group == 0:
                data = [d + SECTION_WEIGHT * r for d, r in zip(data, rolled)]
            dh, dl = split(jnp.concatenate(data, 1))
            table = table_ref.at[2 * half + group]
            high = table[:, :total]
            low = table[:, total:]
            out = (jnp.dot(high, dh, preferred_element_type=F32) + jnp.dot(high, dl, preferred_element_type=F32)
                   + jnp.dot(low, dh, preferred_element_type=F32))
            for c in range(3):
                out_ref[half, :, 3 * group + c] = out[:, c * cz:(c + 1) * cz].reshape(blocks, cy, cz)


def reorder_kernel(lines_ref, local_ref, rate_ref, out_ref):
    problems, comps, cx, cy, cz = local_ref.shape
    on_left = lax.axis_index("gx") == 0
    for x in range(cx):
        k, row = plane_slot(x, on_left)
        for c in range(comps):
            out_ref[:, c, x] = lines_ref[k, :, row + c]
            value = local_ref[:, c, x]
            if x < 3:
                value = value + jnp.where(on_left, lines_ref[x, :, 6 + c], 0.0)
            if x >= cx - 3:
                value = value + jnp.where(on_left, 0.0, lines_ref[x - (cx - 3), :, 6 + c])
            rate_ref[:, c, x] = value


def struct(*shape):
    return jax.ShapeDtypeStruct(shape, F32)


VMEM = pl.BlockSpec(memory_space=pltpu.VMEM)
SMEM = pl.BlockSpec(memory_space=pltpu.SMEM)
PARAMS = pltpu.CompilerParams(vmem_limit_bytes=40 * 1024 * 1024)
STREAMED = pltpu.CompilerParams(vmem_limit_bytes=60 * 1024 * 1024)


def on_device(magnetic, velocity, shear_shift, freq_index):
    problems, comps, cx, cy, cz = magnetic.shape
    nx, ny, nz = lax.axis_size("gx"), lax.axis_size("gy"), lax.axis_size("gz")
    total_x, total_y, total_z = cx * nx, cy * ny, cz * nz
    gx, gy = lax.axis_index("gx"), lax.axis_index("gy")
    lefts = [jnp.asarray(w) for w in left_weights(cx, cy)]
    mains, faces = right_weights(cz)
    mains, faces = [jnp.asarray(w) for w in mains], [jnp.asarray(w) for w in faces]
    pair = 2
    steps = problems // pair

    def whole(array):
        return pl.BlockSpec(array.shape, lambda i: (0,) * len(array.shape))

    def cut(*shape):
        return pl.BlockSpec((pair,) + shape, lambda i: (i,) + (0,) * len(shape))

    tile, face, edge, side = (comps, cx, cy, cz), (comps, 3, cy, cz), (comps, 3, cx, cz), (comps, 8, cx * cy)
    weights = [*lefts, *mains, *faces]
    outs = (tile, face, face, edge, edge, side)
    local, facing, outer, y0, y1, z = pl.pallas_call(
        functools.partial(rates_kernel, total_z=total_z),
        grid=(steps,),
        out_shape=tuple(struct(problems, *shape) for shape in outs),
        in_specs=[SMEM, cut(*tile), whole(velocity)] + [whole(w) for w in weights],
        out_specs=tuple(cut(*shape) for shape in outs),
        compiler_params=STREAMED,
    )(freq_index, magnetic, velocity, *weights)

    swap = [(0, 1), (1, 0)]
    down = [(j, (j - 1) % ny) for j in range(ny)]
    up = [(j, (j + 1) % ny) for j in range(ny)]
    zdown = [(j, (j - 1) % nz) for j in range(nz)]
    zup = [(j, (j + 1) % nz) for j in range(nz)]
    facing_in = lax.ppermute(facing, "gx", swap)
    y0_in = lax.ppermute(y0, "gy", down)
    y1_in = lax.ppermute(y1, "gy", up)
    z_up = lax.ppermute(z, "gz", zdown)
    z_down = lax.ppermute(z, "gz", zup)
    placing = [jnp.asarray(w) for w in place_weights(cx, cy, cz, comps)]
    groups = nx * ny // problems
    rate, lines = pl.pallas_call(
        finish_kernel,
        grid=(steps,),
        out_shape=(struct(problems, *tile), struct(groups, problems, 9, cy, cz)),
        in_specs=[cut(*tile), cut(*tile), cut(*face), cut(*face), cut(*edge), cut(*edge), cut(*side), cut(*side)]
        + [whole(w) for w in placing],
        out_specs=(cut(*tile), pl.BlockSpec((groups, pair, 9, cy, cz), lambda i: (0, i, 0, 0, 0))),
        compiler_params=STREAMED,
    )(magnetic, local, facing_in, outer, y0_in, y1_in, z_up, z_down, *placing)

    matrices = shift_matrices(total_x, total_y)
    order = [[half * cx + planes[half][k] for half in range(2) for planes in (FIRST, SECOND)] for k in range(groups)]
    tables = jnp.asarray(np.stack([matrices[picks] for picks in order]))
    table = lax.dynamic_index_in_dim(tables, (gx * ny + gy) // problems, 0, keepdims=False)
    received = lax.all_to_all(lines.reshape(nx * ny * 9, cy, cz), ("gx", "gy"), 0, 0, tiled=True)
    turned = pl.pallas_call(
        shift_kernel, out_shape=struct(nx, ny, 9, cy, cz), in_specs=[SMEM, VMEM, VMEM], out_specs=VMEM,
        scratch_shapes=[pltpu.VMEM((2 * total_y, cz), F32)], compiler_params=PARAMS,
    )(shear_shift, received.reshape(nx, ny, 9, cy, cz), table)
    returned = lax.all_to_all(turned.reshape(nx * ny * 9, cy, cz), ("gx", "gy"), 0, 0, tiled=True)
    return pl.pallas_call(
        reorder_kernel, out_shape=(struct(problems, *tile),) * 2, in_specs=[VMEM] * 2, out_specs=(VMEM,) * 2,
        compiler_params=PARAMS,
    )(returned.reshape(groups, problems, 9, cy, cz), rate)


def solution(mesh):
    return jax.shard_map(
        on_device,
        mesh=mesh,
        in_specs=(P(None, None, "gx", "gy", "gz"), P(None, "gx", "gy", "gz"), P(), P()),
        out_specs=(P(None, None, "gx", "gy", "gz"), P(None, None, "gx", "gy", "gz")),
        check_vma=False,
    )
```

```python
import functools
import math

import jax
import jax.numpy as jnp
import ml_dtypes
import numpy as np
from jax import lax
from jax.experimental import pallas as pl
from jax.experimental.pallas import tpu as pltpu
from jax.sharding import PartitionSpec as P

SHEAR_RATE = 1.5
TIME_STEP = 0.2
DIFFUSIVITY = 0.1
SECTION_WEIGHT = 1.0 / 3.0

D1 = [TIME_STEP * w / 60.0 for w in (45.0, -9.0, 1.0)]
D2 = [TIME_STEP * DIFFUSIVITY * w / 180.0 for w in (270.0, -27.0, 2.0)]
D2_CENTRE = -TIME_STEP * DIFFUSIVITY * 490.0 / 180.0
STRETCH = -TIME_STEP * SHEAR_RATE

BF16 = jnp.bfloat16
F32 = jnp.float32


def np_split(value):
    value = np.asarray(value, np.float64)
    high = value.astype(np.float32).astype(ml_dtypes.bfloat16)
    low = (value - high.astype(np.float64)).astype(np.float32).astype(ml_dtypes.bfloat16)
    return high, low


def stencil_1d(first_out, outs, size, centre):
    one = np.zeros((outs, size))
    two = np.zeros((outs, size))
    for row in range(outs):
        at = first_out + row
        for d in (1, 2, 3):
            if 0 <= at + d < size:
                one[row, at + d] += D1[d - 1]
                two[row, at + d] += D2[d - 1]
            if 0 <= at - d < size:
                one[row, at - d] -= D1[d - 1]
                two[row, at - d] += D2[d - 1]
        if 0 <= at < size:
            two[row, at] += centre
    return one, two


def left_weights(cx, cy):
    eye_x, eye_y = np.eye(cx), np.eye(cy)
    x1, x2 = stencil_1d(0, cx, cx, D2_CENTRE)
    y1, y2 = stencil_1d(0, cy, cy, D2_CENTRE)
    yl1, yl2 = stencil_1d(-3, 3, cy, 0.0)
    yh1, yh2 = stencil_1d(cy, 3, cy, 0.0)

    def face_y(rows):
        return np.einsum("iy,xz->ixzy", rows, eye_x).reshape(3 * cx, cx * cy)

    none = np.zeros((6 * cx, cx * cy))
    dx = np.concatenate([np.kron(x1, eye_y), none])
    dy = np.concatenate([np.kron(eye_x, y1), face_y(yl1), face_y(yh1)])
    lap = np.concatenate([np.kron(x2, eye_y) + np.kron(eye_x, y2), face_y(yl2), face_y(yh2)])
    out_x = np.concatenate([dy, lap], 1)
    out_y = np.concatenate([-dx, lap], 1)
    out_z = np.concatenate([dx, -dy, lap], 1)
    result = []
    for value in (out_x, out_y, out_z):
        high, low = np_split(value)
        result.append(np.concatenate([high, high, low], 1))
    return result


def right_weights(cz):
    one, two = stencil_1d(0, cz, cz, D2_CENTRE)
    lo1, lo2 = stencil_1d(-3, 3, cz, 0.0)
    hi1, hi2 = stencil_1d(cz, 3, cz, 0.0)
    pad = np.zeros((2, cz))
    face1 = np.concatenate([lo1, hi1, pad])
    face2 = np.concatenate([lo2, hi2, pad])
    mains, faces = [], []
    for main, face in (
        (np.concatenate([-one.T, two.T]), np.concatenate([-face1, face2], 1)),
        (np.concatenate([one.T, two.T]), np.concatenate([face1, face2], 1)),
        (two.T, face2),
    ):
        high, low = np_split(main)
        mains.append(np.concatenate([high, high, low], 0))
        high, low = np_split(face)
        faces.append(np.concatenate([high, high, low], 1))
    return mains, faces


def shift_matrices(total_x, total_y):
    modes = np.arange(total_y // 2 + 1)
    sigma = -SHEAR_RATE * SECTION_WEIGHT * TIME_STEP * (np.arange(total_x) + 0.5 - total_x / 2.0)
    weight = np.full(modes.shape, 2.0)
    weight[0] = 1.0
    away = np.arange(total_y)
    rows = []
    for s in sigma:
        terms = weight[:-1, None] * np.cos(2.0 * np.pi / total_y * modes[:-1, None] * (away[None, :] - s))
        nyquist = np.cos(np.pi * s) * np.cos(np.pi * away)
        rows.append((terms.sum(0) + nyquist) / total_y)
    index = (away[:, None] - away[None, :]) % total_y
    full = np.stack(rows)[:, index]
    high, low = np_split(full)
    return np.concatenate([high, low], 2)


def split(value):
    high = value.astype(BF16)
    low = (value - high.astype(F32)).astype(BF16)
    return high, low


PAIR = 2


def wave_pair(freq_ref, step, cz, total_z):
    position = (lax.axis_index("gz") * cz + lax.broadcasted_iota(jnp.int32, (1, cz), 1)).astype(F32)
    phase = 2.0 * math.pi * freq_ref[step // 2].astype(F32) * position / total_z
    return (jnp.cos(phase), jnp.sin(phase)), step % 2 == 0


def face_sums(m_ref, v_ref, waves, along_x, high, out_ref):
    pair, comps, cx, cy, cz = m_ref.shape
    sign = jnp.where(high, 1.0, -1.0)
    near = [jnp.where(high, cx - 1 - j, j) for j in range(3)]
    flow = [[v_ref[c, x] for c in range(3)] for x in near]
    for i in range(pair):
        add_x = jnp.where(along_x, waves[i], 0.0)
        add_y = jnp.where(along_x, 0.0, waves[i])
        field, turn_y, turn_z = [], [], []
        for x, (vx, vy, vz) in zip(near, flow):
            mx, my, mz = [m_ref[i, c, x] for c in range(3)]
            tx, ty = mx + add_x, my + add_y
            field.append((mx, my, mz))
            turn_y.append(sign * (vz * tx - vx * mz))
            turn_z.append(sign * (vx * ty - vy * tx))
        for n in range(3):
            out = [0.0, 0.0, 0.0]
            for j in range(3 - n):
                one, two = D1[n + j], D2[n + j]
                out[0] += two * field[j][0]
                out[1] += two * field[j][1] + one * turn_z[j]
                out[2] += two * field[j][2] - one * turn_y[j]
            at = jnp.where(high, n, 2 - n)
            for c in range(3):
                out_ref[i, c, at] = out[c]


def block(ref, step):
    return ref.at[pl.ds(step * PAIR, PAIR)]


def facing_kernel(freq_ref, m_ref, v_ref, facing_ref, *, total_z):
    @pl.loop(0, m_ref.shape[0] // PAIR)
    def _(step):
        waves, along_x = wave_pair(freq_ref, step, m_ref.shape[-1], total_z)
        face_sums(block(m_ref, step), v_ref, waves, along_x, lax.axis_index("gx") == 0, block(facing_ref, step))


def rates_kernel(freq_ref, m_ref, v_ref, left_ref, right_ref, face_ref, rate_ref, outer_ref, y0_ref, y1_ref, z_ref, *,
                 total_z):
    cells = m_ref.shape[2] * m_ref.shape[3]

    def part(ref, dim, first, size):
        at = [slice(None), slice(None)]
        at[dim] = pl.ds(first, size)
        return ref.at[tuple(at)]

    first = 0
    lefts = []
    for size in (6 * cells, 6 * cells, 9 * cells):
        lefts.append(part(left_ref, 1, first, size))
        first += size
    first = 0
    cz = m_ref.shape[-1]
    rights, faces = [], []
    for size in (6 * cz, 6 * cz, 3 * cz):
        rights.append(part(right_ref, 0, first, size))
        faces.append(part(face_ref, 1, first, size))
        first += size

    @pl.loop(0, m_ref.shape[0] // PAIR)
    def _(step):
        pair_rates(step, freq_ref, block(m_ref, step), v_ref, *lefts, *rights, *faces,
                   *[block(ref, step) for ref in (rate_ref, outer_ref, y0_ref, y1_ref, z_ref)], total_z=total_z)


def pair_rates(step, freq_ref, m_ref, v_ref, lx_ref, ly_ref, lz_ref, rx_ref, ry_ref, rz_ref, fx_ref, fy_ref, fz_ref,
               rate_ref, outer_ref, y0_ref, y1_ref, z_ref, *, total_z):
    pair, comps, cx, cy, cz = m_ref.shape
    cells = cx * cy
    waves, along_x = wave_pair(freq_ref, step, cz, total_z)
    face_sums(m_ref, v_ref, waves, along_x, lax.axis_index("gx") == 1, outer_ref)

    def wide(parts):
        return jnp.concatenate(parts, 1)

    def tall(value):
        return jnp.concatenate([value[:, i * cz:(i + 1) * cz] for i in range(pair)], 0)

    m = [wide([m_ref[i, c].reshape(cells, cz) for i in range(pair)]) for c in range(3)]
    v = [wide([v_ref[c].reshape(cells, cz)] * pair) for c in range(3)]
    wave = wide(waves)
    tx = m[0] + jnp.where(along_x, wave, 0.0)
    ty = m[1] + jnp.where(along_x, 0.0, wave)
    tz = m[2]
    f = [
        v[1] * tz - v[2] * ty,
        v[2] * tx - v[0] * tz,
        v[0] * ty - v[1] * tx,
    ]
    fh, fl = zip(*[split(a) for a in f])
    mh, ml = zip(*[split(a) for a in m])
    lefts = (
        (lx_ref, [fh[2], mh[0], fl[2], ml[0], fh[2], mh[0]]),
        (ly_ref, [fh[2], mh[1], fl[2], ml[1], fh[2], mh[1]]),
        (lz_ref, [fh[1], fh[0], mh[2], fl[1], fl[0], ml[2], fh[1], fh[0], mh[2]]),
    )
    rights = (
        (rx_ref, fx_ref, [fh[1], mh[0], fl[1], ml[0], fh[1], mh[0]]),
        (ry_ref, fy_ref, [fh[0], mh[1], fl[0], ml[1], fh[0], mh[1]]),
        (rz_ref, fz_ref, [mh[2], ml[2], mh[2]]),
    )
    for c in range(3):
        weights, data = lefts[c]
        left = jnp.dot(weights[...], jnp.concatenate(data, 0), preferred_element_type=F32)
        if c == 1:
            main_left = left[:cells] + STRETCH * tx
        else:
            main_left = left[:cells]
        main, face, data = rights[c]
        data = jnp.concatenate([tall(d) for d in data], 1)
        right = jnp.dot(data, main[...], preferred_element_type=F32)
        ghost = lax.dot_general(face[...], data, (((1,), (1,)), ((), ())), preferred_element_type=F32)
        for i in range(pair):
            lanes = slice(i * cz, (i + 1) * cz)
            rate = main_left[:, lanes] + right[i * cells:(i + 1) * cells]
            rate_ref[i, c] = rate.reshape(cx, cy, cz)
            z_ref[i, c] = ghost[:, i * cells:(i + 1) * cells]
            at = cells
            for ref in (y0_ref, y1_ref):
                ref[i, c] = left[at:at + 3 * cx, lanes].reshape(3, cx, cz)
                at += 3 * cx


def three(value):
    high = value.astype(BF16)
    rest = value - high.astype(F32)
    middle = rest.astype(BF16)
    return [high, middle, (rest - middle.astype(F32)).astype(BF16)]


def place_weights(cx, cy, cz, comps):
    left = np.zeros((cx * cy, 6 * cx))
    for i in range(3):
        for x in range(cx):
            left[x * cy + i, i * cx + x] = 1.0
            left[x * cy + cy - 3 + i, 3 * cx + i * cx + x] = 1.0
    right = np.zeros((8 * comps, comps * cz))
    for c in range(comps):
        for i in range(3):
            right[8 * c + i, c * cz + cz - 3 + i] = 1.0
            right[8 * c + 3 + i, c * cz + i] = 1.0
    return (np.concatenate([left] * 3, 1).astype(ml_dtypes.bfloat16),
            np.concatenate([right] * 3, 0).astype(ml_dtypes.bfloat16))


FIRST = ((0, 1, 2, 6), (5, 6, 7, 3))
SECOND = ((3, 4, 5, 7), (0, 1, 2, 4))


def plane_slot(x, on_left):
    where = []
    for half in range(2):
        if x in FIRST[half]:
            where.append((FIRST[half].index(x), 0))
        else:
            where.append((SECOND[half].index(x), 3))
    return tuple(jnp.where(on_left, a, b) for a, b in zip(*where))


def finish_kernel(m_ref, local_ref, facing_ref, outer_ref, y0_ref, y1_ref, zup_ref, zdown_ref, left_ref, right_ref,
                  rate_ref, lines_ref):
    @pl.loop(0, m_ref.shape[0] // PAIR)
    def _(step):
        refs = (m_ref, local_ref, facing_ref, outer_ref, y0_ref, y1_ref, zup_ref, zdown_ref)
        finish_pair(*[block(ref, step) for ref in refs], left_ref, right_ref, block(rate_ref, step),
                    lines_ref.at[:, pl.ds(step * PAIR, PAIR)])


def finish_pair(m_ref, local_ref, facing_ref, outer_ref, y0_ref, y1_ref, zup_ref, zdown_ref, left_ref, right_ref,
                rate_ref, lines_ref):
    pair, comps, cx, cy, cz = m_ref.shape
    cells = cx * cy
    on_left = lax.axis_index("gx") == 0
    zrow = lax.broadcasted_iota(jnp.int32, (8, cells), 0)
    for i in range(pair):
        ghosts = jnp.concatenate([jnp.where(zrow < 3, zup_ref[i, c], zdown_ref[i, c]) for c in range(comps)], 0)
        ghosts = jnp.concatenate(three(ghosts), 0)
        faces = jnp.concatenate([
            jnp.concatenate([y1_ref[i, c].reshape(3 * cx, cz), y0_ref[i, c].reshape(3 * cx, cz)], 0)
            for c in range(comps)], 1)
        placed = jnp.dot(left_ref[...], jnp.concatenate(three(faces), 0), preferred_element_type=F32)
        placed = placed + lax.dot_general(ghosts, right_ref[...], (((0,), (0,)), ((), ())), preferred_element_type=F32)
        for c in range(comps):
            spread = placed[:, c * cz:(c + 1) * cz].reshape(cx, cy, cz)
            for x in range(cx):
                value = local_ref[i, c, x] + spread[x]
                if x < 3:
                    value = value + jnp.where(on_left, 0.0, facing_ref[i, c, x])
                if x >= cx - 3:
                    value = value + jnp.where(on_left, facing_ref[i, c, x - (cx - 3)], 0.0)
                rate_ref[i, c, x] = value
                k, row = plane_slot(x, on_left)
                lines_ref[k, i, row + c] = m_ref[i, c, x] + SECTION_WEIGHT * value
            for j in range(3):
                lines_ref[j, i, 6 + c] = outer_ref[i, c, j]
            lines_ref[3, i, 6 + c] = jnp.zeros((cy, cz), F32)


def shift_kernel(shift_ref, data_ref, table_ref, out_ref, twice_ref):
    halves, blocks, rows, cy, cz = data_ref.shape
    total = blocks * cy
    for half in range(halves):
        first = shift_ref[0] if half == 0 else (total - shift_ref[1]) & (total - 1)
        rolled = []
        for c in range(3):
            sums = data_ref[1 - half, :, 6 + c].reshape(total, cz)
            twice_ref[0:total] = sums
            twice_ref[total:2 * total] = sums
            moved = twice_ref[pl.ds(first, total), :]
            out_ref[half, :, 6 + c] = moved.reshape(blocks, cy, cz)
            rolled.append(moved)
        for group in range(2):
            data = [data_ref[half, :, 3 * group + c].reshape(total, cz) for c in range(3)]
            if group == 0:
                data = [d + SECTION_WEIGHT * r for d, r in zip(data, rolled)]
            dh, dl = split(jnp.concatenate(data, 1))
            table = table_ref.at[2 * half + group]
            high = table[:, :total]
            low = table[:, total:]
            out = (jnp.dot(high, dh, preferred_element_type=F32) + jnp.dot(high, dl, preferred_element_type=F32)
                   + jnp.dot(low, dh, preferred_element_type=F32))
            for c in range(3):
                out_ref[half, :, 3 * group + c] = out[:, c * cz:(c + 1) * cz].reshape(blocks, cy, cz)


def reorder_kernel(lines_ref, local_ref, rate_ref, out_ref):
    problems, comps, cx, cy, cz = local_ref.shape
    on_left = lax.axis_index("gx") == 0
    for x in range(cx):
        k, row = plane_slot(x, on_left)
        for c in range(comps):
            out_ref[:, c, x] = lines_ref[k, :, row + c]
            value = local_ref[:, c, x]
            if x < 3:
                value = value + jnp.where(on_left, lines_ref[x, :, 6 + c], 0.0)
            if x >= cx - 3:
                value = value + jnp.where(on_left, 0.0, lines_ref[x - (cx - 3), :, 6 + c])
            rate_ref[:, c, x] = value


def struct(*shape):
    return jax.ShapeDtypeStruct(shape, F32)


VMEM = pl.BlockSpec(memory_space=pltpu.VMEM)
SMEM = pl.BlockSpec(memory_space=pltpu.SMEM)
PARAMS = pltpu.CompilerParams(vmem_limit_bytes=32 * 1024 * 1024)


def on_device(magnetic, velocity, shear_shift, freq_index):
    problems, comps, cx, cy, cz = magnetic.shape
    nx, ny, nz = lax.axis_size("gx"), lax.axis_size("gy"), lax.axis_size("gz")
    total_x, total_y, total_z = cx * nx, cy * ny, cz * nz
    gx, gy = lax.axis_index("gx"), lax.axis_index("gy")
    lefts = left_weights(cx, cy)
    mains, faces = right_weights(cz)
    tile, face, edge, side = (comps, cx, cy, cz), (comps, 3, cy, cz), (comps, 3, cx, cz), (comps, 8, cx * cy)
    facing = pl.pallas_call(
        functools.partial(facing_kernel, total_z=total_z),
        out_shape=struct(problems, *face),
        in_specs=[SMEM, VMEM, VMEM], out_specs=VMEM, compiler_params=PARAMS,
    )(freq_index, magnetic, velocity)
    weights = [jnp.asarray(np.concatenate(w, dim)) for w, dim in ((lefts, 1), (mains, 0), (faces, 1))]
    outs = (tile, face, edge, edge, side)
    local, outer, y0, y1, z = pl.pallas_call(
        functools.partial(rates_kernel, total_z=total_z),
        out_shape=tuple(struct(problems, *shape) for shape in outs),
        in_specs=[SMEM] + [VMEM] * 5, out_specs=(VMEM,) * 5, compiler_params=PARAMS,
        cost_estimate=pl.CostEstimate(flops=1 << 30, bytes_accessed=1 << 24, transcendentals=0),
    )(freq_index, magnetic, velocity, *weights)

    swap = [(0, 1), (1, 0)]
    down = [(j, (j - 1) % ny) for j in range(ny)]
    up = [(j, (j + 1) % ny) for j in range(ny)]
    zdown = [(j, (j - 1) % nz) for j in range(nz)]
    zup = [(j, (j + 1) % nz) for j in range(nz)]
    facing_in = lax.ppermute(facing, "gx", swap)
    y0_in = lax.ppermute(y0, "gy", down)
    y1_in = lax.ppermute(y1, "gy", up)
    z_up = lax.ppermute(z, "gz", zdown)
    z_down = lax.ppermute(z, "gz", zup)
    placing = [jnp.asarray(w) for w in place_weights(cx, cy, cz, comps)]
    groups = nx * ny // problems
    rate, lines = pl.pallas_call(
        finish_kernel,
        out_shape=(struct(problems, *tile), struct(groups, problems, 9, cy, cz)),
        in_specs=[VMEM] * 10, out_specs=(VMEM,) * 2, compiler_params=PARAMS,
    )(magnetic, local, facing_in, outer, y0_in, y1_in, z_up, z_down, *placing)

    matrices = shift_matrices(total_x, total_y)
    order = [[half * cx + planes[half][k] for half in range(2) for planes in (FIRST, SECOND)] for k in range(groups)]
    tables = jnp.asarray(np.stack([matrices[picks] for picks in order]))
    table = lax.dynamic_index_in_dim(tables, (gx * ny + gy) // problems, 0, keepdims=False)
    received = lax.all_to_all(lines.reshape(nx * ny * 9, cy, cz), ("gx", "gy"), 0, 0, tiled=True)
    turned = pl.pallas_call(
        shift_kernel, out_shape=struct(nx, ny, 9, cy, cz), in_specs=[SMEM, VMEM, VMEM], out_specs=VMEM,
        scratch_shapes=[pltpu.VMEM((2 * total_y, cz), F32)], compiler_params=PARAMS,
    )(shear_shift, received.reshape(nx, ny, 9, cy, cz), table)
    returned = lax.all_to_all(turned.reshape(nx * ny * 9, cy, cz), ("gx", "gy"), 0, 0, tiled=True)
    return pl.pallas_call(
        reorder_kernel, out_shape=(struct(problems, *tile),) * 2, in_specs=[VMEM] * 2, out_specs=(VMEM,) * 2,
        compiler_params=PARAMS,
    )(returned.reshape(groups, problems, 9, cy, cz), rate)


def solution(mesh):
    return jax.shard_map(
        on_device,
        mesh=mesh,
        in_specs=(P(None, None, "gx", "gy", "gz"), P(None, "gx", "gy", "gz"), P(), P()),
        out_specs=(P(None, None, "gx", "gy", "gz"), P(None, None, "gx", "gy", "gz")),
        check_vma=False,
    )
```

```python
import functools
import math

import jax
import jax.numpy as jnp
import ml_dtypes
import numpy as np
from jax import lax
from jax.experimental import pallas as pl
from jax.experimental.pallas import tpu as pltpu
from jax.sharding import PartitionSpec as P

SHEAR_RATE = 1.5
TIME_STEP = 0.2
DIFFUSIVITY = 0.1
SECTION_WEIGHT = 1.0 / 3.0

D1 = [TIME_STEP * w / 60.0 for w in (45.0, -9.0, 1.0)]
D2 = [TIME_STEP * DIFFUSIVITY * w / 180.0 for w in (270.0, -27.0, 2.0)]
D2_CENTRE = -TIME_STEP * DIFFUSIVITY * 490.0 / 180.0
STRETCH = -TIME_STEP * SHEAR_RATE

BF16 = jnp.bfloat16
F32 = jnp.float32


def np_split(value):
    value = np.asarray(value, np.float64)
    high = value.astype(np.float32).astype(ml_dtypes.bfloat16)
    low = (value - high.astype(np.float64)).astype(np.float32).astype(ml_dtypes.bfloat16)
    return high, low


def stencil_1d(first_out, outs, size, centre):
    one = np.zeros((outs, size))
    two = np.zeros((outs, size))
    for row in range(outs):
        at = first_out + row
        for d in (1, 2, 3):
            if 0 <= at + d < size:
                one[row, at + d] += D1[d - 1]
                two[row, at + d] += D2[d - 1]
            if 0 <= at - d < size:
                one[row, at - d] -= D1[d - 1]
                two[row, at - d] += D2[d - 1]
        if 0 <= at < size:
            two[row, at] += centre
    return one, two


def left_weights(cx, cy):
    eye_x, eye_y = np.eye(cx), np.eye(cy)
    x1, x2 = stencil_1d(0, cx, cx, D2_CENTRE)
    y1, y2 = stencil_1d(0, cy, cy, D2_CENTRE)
    yl1, yl2 = stencil_1d(-3, 3, cy, 0.0)
    yh1, yh2 = stencil_1d(cy, 3, cy, 0.0)

    def face_y(rows):
        return np.einsum("iy,xz->ixzy", rows, eye_x).reshape(3 * cx, cx * cy)

    none = np.zeros((6 * cx, cx * cy))
    dx = np.concatenate([np.kron(x1, eye_y), none])
    dy = np.concatenate([np.kron(eye_x, y1), face_y(yl1), face_y(yh1)])
    lap = np.concatenate([np.kron(x2, eye_y) + np.kron(eye_x, y2), face_y(yl2), face_y(yh2)])
    out_x = np.concatenate([dy, lap], 1)
    out_y = np.concatenate([-dx, lap], 1)
    out_z = np.concatenate([dx, -dy, lap], 1)
    result = []
    for value in (out_x, out_y, out_z):
        high, low = np_split(value)
        result.append(np.concatenate([high, high, low], 1))
    return result


def right_weights(cz):
    one, two = stencil_1d(0, cz, cz, D2_CENTRE)
    lo1, lo2 = stencil_1d(-3, 3, cz, 0.0)
    hi1, hi2 = stencil_1d(cz, 3, cz, 0.0)
    pad = np.zeros((2, cz))
    face1 = np.concatenate([lo1, hi1, pad])
    face2 = np.concatenate([lo2, hi2, pad])
    mains, faces = [], []
    for main, face in (
        (np.concatenate([-one.T, two.T]), np.concatenate([-face1, face2], 1)),
        (np.concatenate([one.T, two.T]), np.concatenate([face1, face2], 1)),
        (two.T, face2),
    ):
        high, low = np_split(main)
        mains.append(np.concatenate([high, high, low], 0))
        high, low = np_split(face)
        faces.append(np.concatenate([high, high, low], 1))
    return mains, faces


def shift_matrices(total_x, total_y):
    modes = np.arange(total_y // 2 + 1)
    sigma = -SHEAR_RATE * SECTION_WEIGHT * TIME_STEP * (np.arange(total_x) + 0.5 - total_x / 2.0)
    weight = np.full(modes.shape, 2.0)
    weight[0] = 1.0
    away = np.arange(total_y)
    rows = []
    for s in sigma:
        terms = weight[:-1, None] * np.cos(2.0 * np.pi / total_y * modes[:-1, None] * (away[None, :] - s))
        nyquist = np.cos(np.pi * s) * np.cos(np.pi * away)
        rows.append((terms.sum(0) + nyquist) / total_y)
    index = (away[:, None] - away[None, :]) % total_y
    full = np.stack(rows)[:, index]
    high, low = np_split(full)
    return np.concatenate([high, low], 2)


def split(value):
    high = value.astype(BF16)
    low = (value - high.astype(F32)).astype(BF16)
    return high, low


PAIR = 2


def wave_pair(freq_ref, step, cz, total_z):
    position = (lax.axis_index("gz") * cz + lax.broadcasted_iota(jnp.int32, (1, cz), 1)).astype(F32)
    phase = 2.0 * math.pi * freq_ref[step // 2].astype(F32) * position / total_z
    return (jnp.cos(phase), jnp.sin(phase)), step % 2 == 0


def face_sums(m_ref, v_ref, waves, along_x, high, out_ref):
    pair, comps, cx, cy, cz = m_ref.shape
    sign = jnp.where(high, 1.0, -1.0)
    near = [jnp.where(high, cx - 1 - j, j) for j in range(3)]
    flow = [[v_ref[c, x] for c in range(3)] for x in near]
    for i in range(pair):
        add_x = jnp.where(along_x, waves[i], 0.0)
        add_y = jnp.where(along_x, 0.0, waves[i])
        field, turn_y, turn_z = [], [], []
        for x, (vx, vy, vz) in zip(near, flow):
            mx, my, mz = [m_ref[i, c, x] for c in range(3)]
            tx, ty = mx + add_x, my + add_y
            field.append((mx, my, mz))
            turn_y.append(sign * (vz * tx - vx * mz))
            turn_z.append(sign * (vx * ty - vy * tx))
        for n in range(3):
            out = [0.0, 0.0, 0.0]
            for j in range(3 - n):
                one, two = D1[n + j], D2[n + j]
                out[0] += two * field[j][0]
                out[1] += two * field[j][1] + one * turn_z[j]
                out[2] += two * field[j][2] - one * turn_y[j]
            at = jnp.where(high, n, 2 - n)
            for c in range(3):
                out_ref[i, c, at] = out[c]


def block(ref, step):
    return ref.at[pl.ds(step * PAIR, PAIR)]


def facing_kernel(freq_ref, m_ref, v_ref, facing_ref, *, total_z):
    @pl.loop(0, m_ref.shape[0] // PAIR)
    def _(step):
        waves, along_x = wave_pair(freq_ref, step, m_ref.shape[-1], total_z)
        face_sums(block(m_ref, step), v_ref, waves, along_x, lax.axis_index("gx") == 0, block(facing_ref, step))


def rates_kernel(freq_ref, m_ref, v_ref, left_ref, right_ref, face_ref, rate_ref, outer_ref, y0_ref, y1_ref, z_ref, *,
                 total_z):
    cells = m_ref.shape[2] * m_ref.shape[3]

    def part(ref, dim, first, size):
        at = [slice(None), slice(None)]
        at[dim] = pl.ds(first, size)
        return ref.at[tuple(at)]

    first = 0
    lefts = []
    for size in (6 * cells, 6 * cells, 9 * cells):
        lefts.append(part(left_ref, 1, first, size))
        first += size
    first = 0
    cz = m_ref.shape[-1]
    rights, faces = [], []
    for size in (6 * cz, 6 * cz, 3 * cz):
        rights.append(part(right_ref, 0, first, size))
        faces.append(part(face_ref, 1, first, size))
        first += size

    @pl.loop(0, m_ref.shape[0] // PAIR)
    def _(step):
        pair_rates(step, freq_ref, block(m_ref, step), v_ref, *lefts, *rights, *faces,
                   *[block(ref, step) for ref in (rate_ref, outer_ref, y0_ref, y1_ref, z_ref)], total_z=total_z)


def pair_rates(step, freq_ref, m_ref, v_ref, lx_ref, ly_ref, lz_ref, rx_ref, ry_ref, rz_ref, fx_ref, fy_ref, fz_ref,
               rate_ref, outer_ref, y0_ref, y1_ref, z_ref, *, total_z):
    pair, comps, cx, cy, cz = m_ref.shape
    cells = cx * cy
    waves, along_x = wave_pair(freq_ref, step, cz, total_z)
    face_sums(m_ref, v_ref, waves, along_x, lax.axis_index("gx") == 1, outer_ref)

    def wide(parts):
        return jnp.concatenate(parts, 1)

    def tall(value):
        return jnp.concatenate([value[:, i * cz:(i + 1) * cz] for i in range(pair)], 0)

    m = [wide([m_ref[i, c].reshape(cells, cz) for i in range(pair)]) for c in range(3)]
    v = [wide([v_ref[c].reshape(cells, cz)] * pair) for c in range(3)]
    wave = wide(waves)
    tx = m[0] + jnp.where(along_x, wave, 0.0)
    ty = m[1] + jnp.where(along_x, 0.0, wave)
    tz = m[2]
    f = [
        v[1] * tz - v[2] * ty,
        v[2] * tx - v[0] * tz,
        v[0] * ty - v[1] * tx,
    ]
    fh, fl = zip(*[split(a) for a in f])
    mh, ml = zip(*[split(a) for a in m])
    lefts = (
        (lx_ref, [fh[2], mh[0], fl[2], ml[0], fh[2], mh[0]]),
        (ly_ref, [fh[2], mh[1], fl[2], ml[1], fh[2], mh[1]]),
        (lz_ref, [fh[1], fh[0], mh[2], fl[1], fl[0], ml[2], fh[1], fh[0], mh[2]]),
    )
    rights = (
        (rx_ref, fx_ref, [fh[1], mh[0], fl[1], ml[0], fh[1], mh[0]]),
        (ry_ref, fy_ref, [fh[0], mh[1], fl[0], ml[1], fh[0], mh[1]]),
        (rz_ref, fz_ref, [mh[2], ml[2], mh[2]]),
    )
    for c in range(3):
        weights, data = lefts[c]
        left = jnp.dot(weights[...], jnp.concatenate(data, 0), preferred_element_type=F32)
        if c == 1:
            main_left = left[:cells] + STRETCH * tx
        else:
            main_left = left[:cells]
        main, face, data = rights[c]
        data = jnp.concatenate([tall(d) for d in data], 1)
        right = jnp.dot(data, main[...], preferred_element_type=F32)
        ghost = lax.dot_general(face[...], data, (((1,), (1,)), ((), ())), preferred_element_type=F32)
        for i in range(pair):
            lanes = slice(i * cz, (i + 1) * cz)
            rate = main_left[:, lanes] + right[i * cells:(i + 1) * cells]
            rate_ref[i, c] = rate.reshape(cx, cy, cz)
            z_ref[i, c] = ghost[:, i * cells:(i + 1) * cells]
            at = cells
            for ref in (y0_ref, y1_ref):
                ref[i, c] = left[at:at + 3 * cx, lanes].reshape(3, cx, cz)
                at += 3 * cx


def three(value):
    high = value.astype(BF16)
    rest = value - high.astype(F32)
    middle = rest.astype(BF16)
    return [high, middle, (rest - middle.astype(F32)).astype(BF16)]


def place_weights(cx, cy, cz, comps):
    left = np.zeros((cx * cy, 6 * cx))
    for i in range(3):
        for x in range(cx):
            left[x * cy + i, i * cx + x] = 1.0
            left[x * cy + cy - 3 + i, 3 * cx + i * cx + x] = 1.0
    right = np.zeros((8 * comps, comps * cz))
    for c in range(comps):
        for i in range(3):
            right[8 * c + i, c * cz + cz - 3 + i] = 1.0
            right[8 * c + 3 + i, c * cz + i] = 1.0
    return (np.concatenate([left] * 3, 1).astype(ml_dtypes.bfloat16),
            np.concatenate([right] * 3, 0).astype(ml_dtypes.bfloat16))


FIRST = ((0, 1, 2, 6), (5, 6, 7, 3))
SECOND = ((3, 4, 5, 7), (0, 1, 2, 4))


def plane_slot(x, on_left):
    where = []
    for half in range(2):
        if x in FIRST[half]:
            where.append((FIRST[half].index(x), 0))
        else:
            where.append((SECOND[half].index(x), 3))
    return tuple(jnp.where(on_left, a, b) for a, b in zip(*where))


def lines_kernel(m_ref, local_ref, facing_ref, outer_ref, y0_ref, y1_ref, zup_ref, zdown_ref, left_ref, right_ref,
                 lines_ref):
    @pl.loop(0, m_ref.shape[0] // PAIR)
    def _(step):
        refs = (m_ref, local_ref, facing_ref, outer_ref, y0_ref, y1_ref, zup_ref, zdown_ref)
        finish_pair(*[block(ref, step) for ref in refs], left_ref, right_ref, None,
                    lines_ref.at[:, pl.ds(step * PAIR, PAIR)])


def section_rate_kernel(local_ref, facing_ref, y0_ref, y1_ref, zup_ref, zdown_ref, left_ref, right_ref, rate_ref):
    @pl.loop(0, local_ref.shape[0] // PAIR)
    def _(step):
        local, facing, *edges = [block(ref, step) for ref in (local_ref, facing_ref, y0_ref, y1_ref, zup_ref, zdown_ref)]
        finish_pair(None, local, facing, None, *edges, left_ref, right_ref, block(rate_ref, step), None)


def finish_pair(m_ref, local_ref, facing_ref, outer_ref, y0_ref, y1_ref, zup_ref, zdown_ref, left_ref, right_ref,
                rate_ref, lines_ref):
    pair, comps, cx, cy, cz = local_ref.shape
    cells = cx * cy
    on_left = lax.axis_index("gx") == 0
    zrow = lax.broadcasted_iota(jnp.int32, (8, cells), 0)
    for i in range(pair):
        ghosts = jnp.concatenate([jnp.where(zrow < 3, zup_ref[i, c], zdown_ref[i, c]) for c in range(comps)], 0)
        ghosts = jnp.concatenate(three(ghosts), 0)
        faces = jnp.concatenate([
            jnp.concatenate([y1_ref[i, c].reshape(3 * cx, cz), y0_ref[i, c].reshape(3 * cx, cz)], 0)
            for c in range(comps)], 1)
        placed = jnp.dot(left_ref[...], jnp.concatenate(three(faces), 0), preferred_element_type=F32)
        placed = placed + lax.dot_general(ghosts, right_ref[...], (((0,), (0,)), ((), ())), preferred_element_type=F32)
        for c in range(comps):
            spread = placed[:, c * cz:(c + 1) * cz].reshape(cx, cy, cz)
            for x in range(cx):
                value = local_ref[i, c, x] + spread[x]
                if x < 3:
                    value = value + jnp.where(on_left, 0.0, facing_ref[i, c, x])
                if x >= cx - 3:
                    value = value + jnp.where(on_left, facing_ref[i, c, x - (cx - 3)], 0.0)
                if lines_ref is None:
                    rate_ref[i, c, x] = value
                else:
                    k, row = plane_slot(x, on_left)
                    lines_ref[k, i, row + c] = m_ref[i, c, x] + SECTION_WEIGHT * value
            if lines_ref is not None:
                for j in range(3):
                    lines_ref[j, i, 6 + c] = outer_ref[i, c, j]
                lines_ref[3, i, 6 + c] = jnp.zeros((cy, cz), F32)


def shift_kernel(shift_ref, data_ref, table_ref, out_ref, twice_ref):
    halves, blocks, rows, cy, cz = data_ref.shape
    total = blocks * cy
    for half in range(halves):
        first = shift_ref[0] if half == 0 else (total - shift_ref[1]) & (total - 1)
        rolled = []
        for c in range(3):
            sums = data_ref[1 - half, :, 6 + c].reshape(total, cz)
            twice_ref[0:total] = sums
            twice_ref[total:2 * total] = sums
            moved = twice_ref[pl.ds(first, total), :]
            out_ref[half, :, 6 + c] = moved.reshape(blocks, cy, cz)
            rolled.append(moved)
        for group in range(2):
            data = [data_ref[half, :, 3 * group + c].reshape(total, cz) for c in range(3)]
            if group == 0:
                data = [d + SECTION_WEIGHT * r for d, r in zip(data, rolled)]
            dh, dl = split(jnp.concatenate(data, 1))
            table = table_ref.at[2 * half + group]
            high = table[:, :total]
            low = table[:, total:]
            out = (jnp.dot(high, dh, preferred_element_type=F32) + jnp.dot(high, dl, preferred_element_type=F32)
                   + jnp.dot(low, dh, preferred_element_type=F32))
            for c in range(3):
                out_ref[half, :, 3 * group + c] = out[:, c * cz:(c + 1) * cz].reshape(blocks, cy, cz)


def reorder_kernel(lines_ref, local_ref, rate_ref, out_ref):
    problems, comps, cx, cy, cz = local_ref.shape
    on_left = lax.axis_index("gx") == 0
    for x in range(cx):
        k, row = plane_slot(x, on_left)
        for c in range(comps):
            out_ref[:, c, x] = lines_ref[k, :, row + c]
            value = local_ref[:, c, x]
            if x < 3:
                value = value + jnp.where(on_left, lines_ref[x, :, 6 + c], 0.0)
            if x >= cx - 3:
                value = value + jnp.where(on_left, 0.0, lines_ref[x - (cx - 3), :, 6 + c])
            rate_ref[:, c, x] = value


def struct(*shape):
    return jax.ShapeDtypeStruct(shape, F32)


VMEM = pl.BlockSpec(memory_space=pltpu.VMEM)
SMEM = pl.BlockSpec(memory_space=pltpu.SMEM)
PARAMS = pltpu.CompilerParams(vmem_limit_bytes=32 * 1024 * 1024)


def on_device(magnetic, velocity, shear_shift, freq_index):
    problems, comps, cx, cy, cz = magnetic.shape
    nx, ny, nz = lax.axis_size("gx"), lax.axis_size("gy"), lax.axis_size("gz")
    total_x, total_y, total_z = cx * nx, cy * ny, cz * nz
    gx, gy = lax.axis_index("gx"), lax.axis_index("gy")
    lefts = left_weights(cx, cy)
    mains, faces = right_weights(cz)
    tile, face, edge, side = (comps, cx, cy, cz), (comps, 3, cy, cz), (comps, 3, cx, cz), (comps, 8, cx * cy)
    facing = pl.pallas_call(
        functools.partial(facing_kernel, total_z=total_z),
        out_shape=struct(problems, *face),
        in_specs=[SMEM, VMEM, VMEM], out_specs=VMEM, compiler_params=PARAMS,
    )(freq_index, magnetic, velocity)
    weights = [jnp.asarray(np.concatenate(w, dim)) for w, dim in ((lefts, 1), (mains, 0), (faces, 1))]
    outs = (tile, face, edge, edge, side)
    local, outer, y0, y1, z = pl.pallas_call(
        functools.partial(rates_kernel, total_z=total_z),
        out_shape=tuple(struct(problems, *shape) for shape in outs),
        in_specs=[SMEM] + [VMEM] * 5, out_specs=(VMEM,) * 5, compiler_params=PARAMS,
        cost_estimate=pl.CostEstimate(flops=1 << 30, bytes_accessed=1 << 24, transcendentals=0),
    )(freq_index, magnetic, velocity, *weights)

    swap = [(0, 1), (1, 0)]
    down = [(j, (j - 1) % ny) for j in range(ny)]
    up = [(j, (j + 1) % ny) for j in range(ny)]
    zdown = [(j, (j - 1) % nz) for j in range(nz)]
    zup = [(j, (j + 1) % nz) for j in range(nz)]
    facing_in = lax.ppermute(facing, "gx", swap)
    y0_in = lax.ppermute(y0, "gy", down)
    y1_in = lax.ppermute(y1, "gy", up)
    z_up = lax.ppermute(z, "gz", zdown)
    z_down = lax.ppermute(z, "gz", zup)
    placing = [jnp.asarray(w) for w in place_weights(cx, cy, cz, comps)]
    groups = nx * ny // problems
    lines = pl.pallas_call(
        lines_kernel, out_shape=struct(groups, problems, 9, cy, cz),
        in_specs=[VMEM] * 10, out_specs=VMEM, compiler_params=PARAMS,
    )(magnetic, local, facing_in, outer, y0_in, y1_in, z_up, z_down, *placing)
    rate = pl.pallas_call(
        section_rate_kernel, out_shape=struct(problems, *tile),
        in_specs=[VMEM] * 8, out_specs=VMEM, compiler_params=PARAMS,
        cost_estimate=pl.CostEstimate(flops=1 << 28, bytes_accessed=1 << 22, transcendentals=0),
    )(local, facing_in, y0_in, y1_in, z_up, z_down, *placing)

    matrices = shift_matrices(total_x, total_y)
    order = [[half * cx + planes[half][k] for half in range(2) for planes in (FIRST, SECOND)] for k in range(groups)]
    tables = jnp.asarray(np.stack([matrices[picks] for picks in order]))
    table = lax.dynamic_index_in_dim(tables, (gx * ny + gy) // problems, 0, keepdims=False)
    received = lax.all_to_all(lines.reshape(nx * ny * 9, cy, cz), ("gx", "gy"), 0, 0, tiled=True)
    received, rate = lax.optimization_barrier((received, rate))
    turned = pl.pallas_call(
        shift_kernel, out_shape=struct(nx, ny, 9, cy, cz), in_specs=[SMEM, VMEM, VMEM], out_specs=VMEM,
        scratch_shapes=[pltpu.VMEM((2 * total_y, cz), F32)], compiler_params=PARAMS,
    )(shear_shift, received.reshape(nx, ny, 9, cy, cz), table)
    returned = lax.all_to_all(turned.reshape(nx * ny * 9, cy, cz), ("gx", "gy"), 0, 0, tiled=True)
    return pl.pallas_call(
        reorder_kernel, out_shape=(struct(problems, *tile),) * 2, in_specs=[VMEM] * 2, out_specs=(VMEM,) * 2,
        compiler_params=PARAMS,
    )(returned.reshape(groups, problems, 9, cy, cz), rate)


def solution(mesh):
    return jax.shard_map(
        on_device,
        mesh=mesh,
        in_specs=(P(None, None, "gx", "gy", "gz"), P(None, "gx", "gy", "gz"), P(), P()),
        out_specs=(P(None, None, "gx", "gy", "gz"), P(None, None, "gx", "gy", "gz")),
        check_vma=False,
    )
```

```python
import functools
import math

import jax
import jax.numpy as jnp
import ml_dtypes
import numpy as np
from jax import lax
from jax.experimental import pallas as pl
from jax.experimental.pallas import tpu as pltpu
from jax.sharding import PartitionSpec as P

SHEAR_RATE = 1.5
TIME_STEP = 0.2
DIFFUSIVITY = 0.1
SECTION_WEIGHT = 1.0 / 3.0

D1 = [TIME_STEP * w / 60.0 for w in (45.0, -9.0, 1.0)]
D2 = [TIME_STEP * DIFFUSIVITY * w / 180.0 for w in (270.0, -27.0, 2.0)]
D2_CENTRE = -TIME_STEP * DIFFUSIVITY * 490.0 / 180.0
STRETCH = -TIME_STEP * SHEAR_RATE

BF16 = jnp.bfloat16
F32 = jnp.float32


def np_split(value):
    value = np.asarray(value, np.float64)
    high = value.astype(np.float32).astype(ml_dtypes.bfloat16)
    low = (value - high.astype(np.float64)).astype(np.float32).astype(ml_dtypes.bfloat16)
    return high, low


def stencil_1d(first_out, outs, size, centre):
    one = np.zeros((outs, size))
    two = np.zeros((outs, size))
    for row in range(outs):
        at = first_out + row
        for d in (1, 2, 3):
            if 0 <= at + d < size:
                one[row, at + d] += D1[d - 1]
                two[row, at + d] += D2[d - 1]
            if 0 <= at - d < size:
                one[row, at - d] -= D1[d - 1]
                two[row, at - d] += D2[d - 1]
        if 0 <= at < size:
            two[row, at] += centre
    return one, two


def left_weights(cx, cy):
    eye_x, eye_y = np.eye(cx), np.eye(cy)
    x1, x2 = stencil_1d(0, cx, cx, D2_CENTRE)
    y1, y2 = stencil_1d(0, cy, cy, D2_CENTRE)
    yl1, yl2 = stencil_1d(-3, 3, cy, 0.0)
    yh1, yh2 = stencil_1d(cy, 3, cy, 0.0)

    def face_y(rows):
        return np.einsum("iy,xz->ixzy", rows, eye_x).reshape(3 * cx, cx * cy)

    none = np.zeros((6 * cx, cx * cy))
    dx = np.concatenate([np.kron(x1, eye_y), none])
    dy = np.concatenate([np.kron(eye_x, y1), face_y(yl1), face_y(yh1)])
    lap = np.concatenate([np.kron(x2, eye_y) + np.kron(eye_x, y2), face_y(yl2), face_y(yh2)])
    out_x = np.concatenate([dy, lap], 1)
    out_y = np.concatenate([-dx, lap], 1)
    out_z = np.concatenate([dx, -dy, lap], 1)
    result = []
    for value in (out_x, out_y, out_z):
        high, low = np_split(value)
        result.append(np.concatenate([high, high, low], 1))
    return result


def right_weights(cz):
    one, two = stencil_1d(0, cz, cz, D2_CENTRE)
    lo1, lo2 = stencil_1d(-3, 3, cz, 0.0)
    hi1, hi2 = stencil_1d(cz, 3, cz, 0.0)
    pad = np.zeros((2, cz))
    face1 = np.concatenate([lo1, hi1, pad])
    face2 = np.concatenate([lo2, hi2, pad])
    mains, faces = [], []
    for main, face in (
        (np.concatenate([-one.T, two.T]), np.concatenate([-face1, face2], 1)),
        (np.concatenate([one.T, two.T]), np.concatenate([face1, face2], 1)),
        (two.T, face2),
    ):
        high, low = np_split(main)
        mains.append(np.concatenate([high, high, low], 0))
        high, low = np_split(face)
        faces.append(np.concatenate([high, high, low], 1))
    return mains, faces


def shift_matrices(total_x, total_y):
    modes = np.arange(total_y // 2 + 1)
    sigma = -SHEAR_RATE * SECTION_WEIGHT * TIME_STEP * (np.arange(total_x) + 0.5 - total_x / 2.0)
    weight = np.full(modes.shape, 2.0)
    weight[0] = 1.0
    away = np.arange(total_y)
    rows = []
    for s in sigma:
        terms = weight[:-1, None] * np.cos(2.0 * np.pi / total_y * modes[:-1, None] * (away[None, :] - s))
        nyquist = np.cos(np.pi * s) * np.cos(np.pi * away)
        rows.append((terms.sum(0) + nyquist) / total_y)
    index = (away[:, None] - away[None, :]) % total_y
    full = np.stack(rows)[:, index]
    high, low = np_split(full)
    return np.concatenate([high, low], 2)


def split(value):
    high = value.astype(BF16)
    low = (value - high.astype(F32)).astype(BF16)
    return high, low


PAIR = 2


def wave_pair(freq_ref, step, cz, total_z):
    position = (lax.axis_index("gz") * cz + lax.broadcasted_iota(jnp.int32, (1, cz), 1)).astype(F32)
    phase = 2.0 * math.pi * freq_ref[step // 2].astype(F32) * position / total_z
    return (jnp.cos(phase), jnp.sin(phase)), step % 2 == 0


def near_plane(high, j, cx):
    return jnp.where(high, cx - 1 - j, j)


def face_sums(field_of, flow, waves, along_x, high, out_ref):
    pair = out_ref.shape[0]
    sign = jnp.where(high, 1.0, -1.0)
    for i in range(pair):
        add_x = jnp.where(along_x, waves[i], 0.0)
        add_y = jnp.where(along_x, 0.0, waves[i])
        field, turn_y, turn_z = [], [], []
        for j, (vx, vy, vz) in enumerate(flow):
            mx, my, mz = [field_of(i, c, j) for c in range(3)]
            tx, ty = mx + add_x, my + add_y
            field.append((mx, my, mz))
            turn_y.append(sign * (vz * tx - vx * mz))
            turn_z.append(sign * (vx * ty - vy * tx))
        for n in range(3):
            out = [0.0, 0.0, 0.0]
            for j in range(3 - n):
                one, two = D1[n + j], D2[n + j]
                out[0] += two * field[j][0]
                out[1] += two * field[j][1] + one * turn_z[j]
                out[2] += two * field[j][2] - one * turn_y[j]
            at = jnp.where(high, n, 2 - n)
            for c in range(3):
                out_ref[i, c, at] = out[c]


def block(ref, step):
    return ref.at[pl.ds(step * PAIR, PAIR)]


def facing_kernel(freq_ref, m_ref, v_ref, facing_ref, field_ref, flow_ref, sems, *, total_z):
    cx = m_ref.shape[2]
    high = lax.axis_index("gx") == 0
    first = jnp.where(high, cx - 3, 0)
    steps = m_ref.shape[0] // PAIR
    flow_copy = pltpu.make_async_copy(v_ref.at[:, pl.ds(first, 3)], flow_ref, sems.at[steps])
    flow_copy.start()
    copies = []
    for step in range(steps):
        at = pl.ds(step * PAIR, PAIR)
        copies.append(pltpu.make_async_copy(m_ref.at[at, :, pl.ds(first, 3)], field_ref.at[at], sems.at[step]))
        copies[-1].start()
    near = [near_plane(high, j, 3) for j in range(3)]
    waves = [wave_pair(freq_ref, step, m_ref.shape[-1], total_z) for step in range(steps)]
    flow_copy.wait()
    flow = [[flow_ref[c, x] for c in range(3)] for x in near]
    for step in range(steps):
        copies[step].wait()
        mine = block(field_ref, step)
        face_sums(lambda i, c, j: mine[i, c, near[j]], flow, waves[step][0], waves[step][1], high,
                  block(facing_ref, step))


def rates_kernel(freq_ref, m_ref, v_ref, left_ref, right_ref, face_ref, rate_ref, outer_ref, y0_ref, y1_ref, z_ref, *,
                 total_z):
    cells = m_ref.shape[2] * m_ref.shape[3]

    def part(ref, dim, first, size):
        at = [slice(None), slice(None)]
        at[dim] = pl.ds(first, size)
        return ref.at[tuple(at)]

    first = 0
    lefts = []
    for size in (6 * cells, 6 * cells, 9 * cells):
        lefts.append(part(left_ref, 1, first, size))
        first += size
    first = 0
    cz = m_ref.shape[-1]
    rights, faces = [], []
    for size in (6 * cz, 6 * cz, 3 * cz):
        rights.append(part(right_ref, 0, first, size))
        faces.append(part(face_ref, 1, first, size))
        first += size

    @pl.loop(0, m_ref.shape[0] // PAIR)
    def _(step):
        pair_rates(step, freq_ref, block(m_ref, step), v_ref, *lefts, *rights, *faces,
                   *[block(ref, step) for ref in (rate_ref, outer_ref, y0_ref, y1_ref, z_ref)], total_z=total_z)


def pair_rates(step, freq_ref, m_ref, v_ref, lx_ref, ly_ref, lz_ref, rx_ref, ry_ref, rz_ref, fx_ref, fy_ref, fz_ref,
               rate_ref, outer_ref, y0_ref, y1_ref, z_ref, *, total_z):
    pair, comps, cx, cy, cz = m_ref.shape
    cells = cx * cy
    waves, along_x = wave_pair(freq_ref, step, cz, total_z)
    high = lax.axis_index("gx") == 1
    near = [near_plane(high, j, cx) for j in range(3)]
    flow = [[v_ref[c, x] for c in range(3)] for x in near]
    face_sums(lambda i, c, j: m_ref[i, c, near[j]], flow, waves, along_x, high, outer_ref)

    def wide(parts):
        return jnp.concatenate(parts, 1)

    def tall(value):
        return jnp.concatenate([value[:, i * cz:(i + 1) * cz] for i in range(pair)], 0)

    m = [wide([m_ref[i, c].reshape(cells, cz) for i in range(pair)]) for c in range(3)]
    v = [wide([v_ref[c].reshape(cells, cz)] * pair) for c in range(3)]
    wave = wide(waves)
    tx = m[0] + jnp.where(along_x, wave, 0.0)
    ty = m[1] + jnp.where(along_x, 0.0, wave)
    tz = m[2]
    f = [
        v[1] * tz - v[2] * ty,
        v[2] * tx - v[0] * tz,
        v[0] * ty - v[1] * tx,
    ]
    fh, fl = zip(*[split(a) for a in f])
    mh, ml = zip(*[split(a) for a in m])
    lefts = (
        (lx_ref, [fh[2], mh[0], fl[2], ml[0], fh[2], mh[0]]),
        (ly_ref, [fh[2], mh[1], fl[2], ml[1], fh[2], mh[1]]),
        (lz_ref, [fh[1], fh[0], mh[2], fl[1], fl[0], ml[2], fh[1], fh[0], mh[2]]),
    )
    rights = (
        (rx_ref, fx_ref, [fh[1], mh[0], fl[1], ml[0], fh[1], mh[0]]),
        (ry_ref, fy_ref, [fh[0], mh[1], fl[0], ml[1], fh[0], mh[1]]),
        (rz_ref, fz_ref, [mh[2], ml[2], mh[2]]),
    )
    for c in range(3):
        weights, data = lefts[c]
        left = jnp.dot(weights[...], jnp.concatenate(data, 0), preferred_element_type=F32)
        if c == 1:
            main_left = left[:cells] + STRETCH * tx
        else:
            main_left = left[:cells]
        main, face, data = rights[c]
        data = jnp.concatenate([tall(d) for d in data], 1)
        right = jnp.dot(data, main[...], preferred_element_type=F32)
        ghost = lax.dot_general(face[...], data, (((1,), (1,)), ((), ())), preferred_element_type=F32)
        for i in range(pair):
            lanes = slice(i * cz, (i + 1) * cz)
            rate = main_left[:, lanes] + right[i * cells:(i + 1) * cells]
            rate_ref[i, c] = rate.reshape(cx, cy, cz)
            z_ref[i, c] = ghost[:, i * cells:(i + 1) * cells]
            at = cells
            for ref in (y0_ref, y1_ref):
                ref[i, c] = left[at:at + 3 * cx, lanes].reshape(3, cx, cz)
                at += 3 * cx


def three(value):
    high = value.astype(BF16)
    rest = value - high.astype(F32)
    middle = rest.astype(BF16)
    return [high, middle, (rest - middle.astype(F32)).astype(BF16)]


def place_weights(cx, cy, cz, comps):
    left = np.zeros((cx * cy, 6 * cx))
    for i in range(3):
        for x in range(cx):
            left[x * cy + i, i * cx + x] = 1.0
            left[x * cy + cy - 3 + i, 3 * cx + i * cx + x] = 1.0
    right = np.zeros((8 * comps, comps * cz))
    for c in range(comps):
        for i in range(3):
            right[8 * c + i, c * cz + cz - 3 + i] = 1.0
            right[8 * c + 3 + i, c * cz + i] = 1.0
    return (np.concatenate([left] * 3, 1).astype(ml_dtypes.bfloat16),
            np.concatenate([right] * 3, 0).astype(ml_dtypes.bfloat16))


FIRST = ((0, 1, 2, 6), (5, 6, 7, 3))
SECOND = ((3, 4, 5, 7), (0, 1, 2, 4))


def plane_slot(x, on_left):
    where = []
    for half in range(2):
        if x in FIRST[half]:
            where.append((FIRST[half].index(x), 0))
        else:
            where.append((SECOND[half].index(x), 3))
    return tuple(jnp.where(on_left, a, b) for a, b in zip(*where))


def lines_kernel(m_ref, local_ref, facing_ref, outer_ref, y0_ref, y1_ref, zup_ref, zdown_ref, left_ref, right_ref,
                 lines_ref):
    @pl.loop(0, m_ref.shape[0] // PAIR)
    def _(step):
        refs = (m_ref, local_ref, facing_ref, outer_ref, y0_ref, y1_ref, zup_ref, zdown_ref)
        finish_pair(*[block(ref, step) for ref in refs], left_ref, right_ref, None,
                    lines_ref.at[:, pl.ds(step * PAIR, PAIR)])


def section_rate_kernel(local_ref, facing_ref, y0_ref, y1_ref, zup_ref, zdown_ref, left_ref, right_ref, rate_ref):
    @pl.loop(0, local_ref.shape[0] // PAIR)
    def _(step):
        local, facing, *edges = [block(ref, step) for ref in (local_ref, facing_ref, y0_ref, y1_ref, zup_ref, zdown_ref)]
        finish_pair(None, local, facing, None, *edges, left_ref, right_ref, block(rate_ref, step), None)


def finish_pair(m_ref, local_ref, facing_ref, outer_ref, y0_ref, y1_ref, zup_ref, zdown_ref, left_ref, right_ref,
                rate_ref, lines_ref):
    pair, comps, cx, cy, cz = local_ref.shape
    cells = cx * cy
    on_left = lax.axis_index("gx") == 0
    zrow = lax.broadcasted_iota(jnp.int32, (8, cells), 0)
    for i in range(pair):
        ghosts = jnp.concatenate([jnp.where(zrow < 3, zup_ref[i, c], zdown_ref[i, c]) for c in range(comps)], 0)
        ghosts = jnp.concatenate(three(ghosts), 0)
        faces = jnp.concatenate([
            jnp.concatenate([y1_ref[i, c].reshape(3 * cx, cz), y0_ref[i, c].reshape(3 * cx, cz)], 0)
            for c in range(comps)], 1)
        placed = jnp.dot(left_ref[...], jnp.concatenate(three(faces), 0), preferred_element_type=F32)
        placed = placed + lax.dot_general(ghosts, right_ref[...], (((0,), (0,)), ((), ())), preferred_element_type=F32)
        for c in range(comps):
            spread = placed[:, c * cz:(c + 1) * cz].reshape(cx, cy, cz)
            for x in range(cx):
                value = local_ref[i, c, x] + spread[x]
                if x < 3:
                    value = value + jnp.where(on_left, 0.0, facing_ref[i, c, x])
                if x >= cx - 3:
                    value = value + jnp.where(on_left, facing_ref[i, c, x - (cx - 3)], 0.0)
                if lines_ref is None:
                    rate_ref[i, c, x] = value
                else:
                    k, row = plane_slot(x, on_left)
                    lines_ref[k, i, row + c] = m_ref[i, c, x] + SECTION_WEIGHT * value
            if lines_ref is not None:
                for j in range(3):
                    lines_ref[j, i, 6 + c] = outer_ref[i, c, j]
                lines_ref[3, i, 6 + c] = jnp.zeros((cy, cz), F32)


def shift_kernel(shift_ref, data_ref, table_ref, out_ref, twice_ref):
    halves, blocks, rows, cy, cz = data_ref.shape
    total = blocks * cy
    for half in range(halves):
        first = shift_ref[0] if half == 0 else (total - shift_ref[1]) & (total - 1)
        rolled = []
        for c in range(3):
            sums = data_ref[1 - half, :, 6 + c].reshape(total, cz)
            twice_ref[0:total] = sums
            twice_ref[total:2 * total] = sums
            moved = twice_ref[pl.ds(first, total), :]
            out_ref[half, :, 6 + c] = moved.reshape(blocks, cy, cz)
            rolled.append(moved)
        for group in range(2):
            data = [data_ref[half, :, 3 * group + c].reshape(total, cz) for c in range(3)]
            if group == 0:
                data = [d + SECTION_WEIGHT * r for d, r in zip(data, rolled)]
            dh, dl = split(jnp.concatenate(data, 1))
            table = table_ref.at[2 * half + group]
            high = table[:, :total]
            low = table[:, total:]
            out = (jnp.dot(high, dh, preferred_element_type=F32) + jnp.dot(high, dl, preferred_element_type=F32)
                   + jnp.dot(low, dh, preferred_element_type=F32))
            for c in range(3):
                out_ref[half, :, 3 * group + c] = out[:, c * cz:(c + 1) * cz].reshape(blocks, cy, cz)


def reorder_kernel(lines_ref, local_ref, rate_ref, out_ref):
    problems, comps, cx, cy, cz = local_ref.shape
    on_left = lax.axis_index("gx") == 0
    for x in range(cx):
        k, row = plane_slot(x, on_left)
        for c in range(comps):
            out_ref[:, c, x] = lines_ref[k, :, row + c]
            value = local_ref[:, c, x]
            if x < 3:
                value = value + jnp.where(on_left, lines_ref[x, :, 6 + c], 0.0)
            if x >= cx - 3:
                value = value + jnp.where(on_left, 0.0, lines_ref[x - (cx - 3), :, 6 + c])
            rate_ref[:, c, x] = value


def struct(*shape):
    return jax.ShapeDtypeStruct(shape, F32)


VMEM = pl.BlockSpec(memory_space=pltpu.VMEM)
ANY = pl.BlockSpec(memory_space=pl.ANY)
SMEM = pl.BlockSpec(memory_space=pltpu.SMEM)
PARAMS = pltpu.CompilerParams(vmem_limit_bytes=32 * 1024 * 1024)


def on_device(magnetic, velocity, shear_shift, freq_index):
    problems, comps, cx, cy, cz = magnetic.shape
    nx, ny, nz = lax.axis_size("gx"), lax.axis_size("gy"), lax.axis_size("gz")
    total_x, total_y, total_z = cx * nx, cy * ny, cz * nz
    gx, gy = lax.axis_index("gx"), lax.axis_index("gy")
    lefts = left_weights(cx, cy)
    mains, faces = right_weights(cz)
    tile, face, edge, side = (comps, cx, cy, cz), (comps, 3, cy, cz), (comps, 3, cx, cz), (comps, 8, cx * cy)
    facing = pl.pallas_call(
        functools.partial(facing_kernel, total_z=total_z),
        out_shape=struct(problems, *face),
        in_specs=[SMEM, ANY, ANY], out_specs=VMEM,
        compiler_params=pltpu.CompilerParams(vmem_limit_bytes=60 * 1024 * 1024),
        scratch_shapes=[pltpu.VMEM((problems, comps, 3, cy, cz), F32), pltpu.VMEM((comps, 3, cy, cz), F32),
                        pltpu.SemaphoreType.DMA((problems // PAIR + 1,))],
    )(freq_index, magnetic, velocity)
    weights = [jnp.asarray(np.concatenate(w, dim)) for w, dim in ((lefts, 1), (mains, 0), (faces, 1))]
    outs = (tile, face, edge, edge, side)
    local, outer, y0, y1, z = pl.pallas_call(
        functools.partial(rates_kernel, total_z=total_z),
        out_shape=tuple(struct(problems, *shape) for shape in outs),
        in_specs=[SMEM] + [VMEM] * 5, out_specs=(VMEM,) * 5, compiler_params=PARAMS,
        cost_estimate=pl.CostEstimate(flops=1 << 30, bytes_accessed=1 << 24, transcendentals=0),
    )(freq_index, magnetic, velocity, *weights)

    swap = [(0, 1), (1, 0)]
    down = [(j, (j - 1) % ny) for j in range(ny)]
    up = [(j, (j + 1) % ny) for j in range(ny)]
    zdown = [(j, (j - 1) % nz) for j in range(nz)]
    zup = [(j, (j + 1) % nz) for j in range(nz)]
    facing_in = lax.ppermute(facing, "gx", swap)
    y0_in = lax.ppermute(y0, "gy", down)
    y1_in = lax.ppermute(y1, "gy", up)
    z_up = lax.ppermute(z, "gz", zdown)
    z_down = lax.ppermute(z, "gz", zup)
    placing = [jnp.asarray(w) for w in place_weights(cx, cy, cz, comps)]
    groups = nx * ny // problems
    lines = pl.pallas_call(
        lines_kernel, out_shape=struct(groups, problems, 9, cy, cz),
        in_specs=[VMEM] * 10, out_specs=VMEM, compiler_params=PARAMS,
    )(magnetic, local, facing_in, outer, y0_in, y1_in, z_up, z_down, *placing)
    rate = pl.pallas_call(
        section_rate_kernel, out_shape=struct(problems, *tile),
        in_specs=[VMEM] * 8, out_specs=VMEM, compiler_params=PARAMS,
        cost_estimate=pl.CostEstimate(flops=1 << 28, bytes_accessed=1 << 22, transcendentals=0),
    )(local, facing_in, y0_in, y1_in, z_up, z_down, *placing)

    matrices = shift_matrices(total_x, total_y)
    order = [[half * cx + planes[half][k] for half in range(2) for planes in (FIRST, SECOND)] for k in range(groups)]
    tables = jnp.asarray(np.stack([matrices[picks] for picks in order]))
    table = lax.dynamic_index_in_dim(tables, (gx * ny + gy) // problems, 0, keepdims=False)
    received = lax.all_to_all(lines.reshape(nx * ny * 9, cy, cz), ("gx", "gy"), 0, 0, tiled=True)
    received, rate = lax.optimization_barrier((received, rate))
    turned = pl.pallas_call(
        shift_kernel, out_shape=struct(nx, ny, 9, cy, cz), in_specs=[SMEM, VMEM, VMEM], out_specs=VMEM,
        scratch_shapes=[pltpu.VMEM((2 * total_y, cz), F32)], compiler_params=PARAMS,
    )(shear_shift, received.reshape(nx, ny, 9, cy, cz), table)
    returned = lax.all_to_all(turned.reshape(nx * ny * 9, cy, cz), ("gx", "gy"), 0, 0, tiled=True)
    return pl.pallas_call(
        reorder_kernel, out_shape=(struct(problems, *tile),) * 2, in_specs=[VMEM] * 2, out_specs=(VMEM,) * 2,
        compiler_params=PARAMS,
    )(returned.reshape(groups, problems, 9, cy, cz), rate)


def solution(mesh):
    return jax.shard_map(
        on_device,
        mesh=mesh,
        in_specs=(P(None, None, "gx", "gy", "gz"), P(None, "gx", "gy", "gz"), P(), P()),
        out_specs=(P(None, None, "gx", "gy", "gz"), P(None, None, "gx", "gy", "gz")),
        check_vma=False,
    )
```
